256 devices in a mesh: ctx: 16 (over y, x_hi, core), tp: 16 (over z, x_lo).
Axes of the slice: x: 4 (x_hi: 2, x_lo: 2; x = x_hi * 2 + x_lo), y: 4, z: 8, core: 2. Of those that a mesh axis runs over, the one named last changes fastest.
Arguments:
- stream: bfloat16 [6144, 8192], P('ctx', 'tp'), may hold values from -40 to 40
- pending: bfloat16 [16, 6144, 8192], P('tp', 'ctx'), may hold values from -5 to 5
- norm_gain: bfloat16 [8192], replicated, may hold values from 0.099609375 to 1.8984375
- w_query: bfloat16 [8192, 4096], P('ctx', 'tp'), may hold values from -0.0625 to 0.0625
- w_key: bfloat16 [8192, 1024], P('ctx'), may hold values from -0.375 to 0.375
- w_value: bfloat16 [8192, 1024], P('ctx'), may hold values from -0.1875 to 0.1875
- w_out: bfloat16 [4096, 8192], P('tp', 'ctx'), may hold values from -0.09375 to 0.09375
- prefix_keys: bfloat16 [8, 12288, 128], P(None, 'ctx'), may hold values from -600 to 600
- prefix_values: bfloat16 [8, 12288, 128], P(None, 'ctx'), may hold values from -6 to 6
- prefix_segments: int32 [12288], P('ctx'), may hold values from 0 to 15, never falling along the last dimension, each value on 1 to 1536 neighbouring positions
- stretch_segments: int32 [6144], P('ctx'), may hold values from 0 to 15, never falling along the last dimension, each value on 1 to 768 neighbouring positions
- stretch_offset: int32 [1], replicated, may hold values from 12288 to 24575
Outputs:
- output: bfloat16 [6144, 8192], P('ctx', 'tp')
The draws below stay inside these ranges and needn't reach their ends.
Inputs may be any that keep to these rules, and one draw needn't show every extreme that they name: `prefix_segments`: never falls along the positions; every trajectory 0 to 15 occurs. `stretch_segments`: never falls along the positions; every trajectory 0 to 15 occurs.
All inputs are finite; a program needn't handle non-finite values.
Results may differ from the reference program's by a relative error of at most 0.024.
Values may be sent and summed in bfloat16 or wider, within the bound.
A program may use at most 256 MiB of HBM per device.

```python
import math
import jax
import jax.numpy as jnp
import numpy as np
from jax import lax

D = 8192
HQ = 32
KVH = 8
HD = 128
NTRAJ = 16
STRETCH = 6144
PREFIX = 12288
N_TP = 16


def draw_stream(key, part):
    key = jax.random.fold_in(key, 7)
    base_key, row_key, col_key = jax.random.split(key, 3)
    column_trend = 3.0 ** (jnp.arange(D, dtype=jnp.float32) / D)
    spread = jnp.exp(math.log(3.0) * (jax.random.uniform(col_key, (D,), jnp.float32) - 0.5))
    base_draw = jnp.clip(jax.random.normal(base_key, (STRETCH, D), jnp.float32), -6.0, 6.0)
    row_scale = jnp.exp(math.log(10.0) * jax.random.uniform(row_key, (STRETCH, 1), jnp.float32))
    return (0.1 * base_draw * row_scale * column_trend * spread).astype(jnp.bfloat16)


def draw_prefix_keys(key, part):
    key = jax.random.fold_in(key, 13)
    base_key = jax.random.fold_in(key, 0)
    key_shape = (KVH, PREFIX, HD)
    return (3.0 * jnp.clip(jax.random.normal(base_key, key_shape, jnp.float32), -6.0, 6.0)).astype(jnp.bfloat16)


def with_spikes(entries, key, source, target, blocks, factor):
    owner, partner = [(jnp.arange(entries.shape[axis_at]) // (entries.shape[axis_at] // blocks)).reshape([-1 if axis == axis_at else 1 for axis in range(entries.ndim)]) for axis_at in (source, target)]
    chosen = jax.random.permutation(key, blocks)[partner]
    strong = (owner == chosen) | (owner == (partner + blocks // 2) % blocks)
    return jnp.where(strong, factor * entries, entries)


def steps_of(own_key, shape, cuts, smallest, largest):
    loudness, own = 1.0, jax.random.fold_in(own_key, 6)
    for axis_at, parts in cuts:
        steps = jnp.exp(jax.random.uniform(jax.random.fold_in(own, axis_at), (parts,), jnp.float32, smallest / len(cuts), largest / len(cuts)))
        loudness = loudness * jnp.repeat(steps, shape[axis_at] // parts).reshape([-1 if axis == axis_at else 1 for axis in range(len(shape))])
    return loudness


def length_profile(count, total, limit, skew):
    loads = [(1 << 20) // math.isqrt(rank ** skew) + 1 for rank in range(2, count + 1)]
    surplus, given = total - limit - (count - 1), [1] * (count - 1)
    while surplus > 0:
        movable = [i for i in range(count - 1) if given[i] < limit]
        mass, remaining = sum([loads[i] for i in movable]), surplus
        for i in movable:
            more = min(limit - given[i], max(1, remaining * loads[i] // mass), surplus)
            given[i] = given[i] + more
            surplus = surplus - more
    return np.array([limit] + given)


def uneven_parts(own_key, amount, total, most, slope):
    if amount == 2:
        one = jax.random.randint(own_key, (), max(1, total - most), min(most, total - 1) + 1)
        return jnp.stack([one, total - one])
    lengths = jnp.asarray(length_profile(amount, total, most, slope), jnp.int32)
    pairs = (amount - 1) // 2
    giver, sink = lengths[1:1 + 2 * pairs:2], lengths[2:2 + 2 * pairs:2]
    margin = jnp.minimum(giver - 1, most - sink)
    passed = jax.random.randint(jax.random.fold_in(own_key, 1), (pairs,), 0, 1 << 20) % (margin + 1)
    lengths = lengths.at[1:1 + 2 * pairs:2].set(giver - passed).at[2:2 + 2 * pairs:2].set(sink + passed)
    return lengths[jax.random.permutation(jax.random.fold_in(own_key, 2), amount)]


def centred(own_key, shape, scale, reach, pieces=(), kind=jnp.bfloat16):
    gain = steps_of(own_key, shape, pieces, -0.22, 0.18) if pieces else 1.0
    entries = jax.random.normal(own_key, shape, jnp.float32) * scale * gain
    return jnp.minimum(jnp.maximum(entries, -reach), reach).astype(kind)


def heavy_noise(own_key, dims, scale, bound, cuts, heavy, kind=jnp.bfloat16):
    drawn = scale * jax.random.normal(own_key, dims, jnp.float32)
    if cuts:
        drawn = drawn * steps_of(own_key, dims, cuts, -0.22, 0.18)
    return jnp.clip(with_spikes(drawn, jax.random.fold_in(own_key, 3), *heavy), -bound, bound).astype(kind)


def setup_inputs(seed: int = 0) -> dict:
    splits = jax.random.split(jax.random.key(seed), 13)
    return {
        "stream": draw_stream(jax.random.fold_in(splits[12], 71), 0),
        "pending": heavy_noise(splits[1], (N_TP, STRETCH, D), 0.25, 5.0, ((0, 16), (1, 16)), (0, 2, 16, 2.0)),
        "norm_gain": jnp.clip(1.0 + 0.18 * jax.random.normal(splits[2], (D,), jnp.float32), 0.099609375, 1.8984375).astype(jnp.bfloat16),
        "w_query": centred(splits[3], (D, HQ * HD), D ** -0.5, 0.0625, ((0, 16), (1, 16))),
        "w_key": centred(splits[4], (D, KVH * HD), (D // 36) ** -0.5, 0.375, ((0, 16),)),
        "w_value": centred(splits[5], (D, KVH * HD), (D // 9) ** -0.5, 0.1875, ((0, 16),)),
        "w_out": centred(splits[6], (HQ * HD, D), (HQ * HD) ** -0.5, 0.09375, ((0, 16), (1, 16))),
        "prefix_keys": draw_prefix_keys(jax.random.fold_in(splits[12], 71), 0),
        "prefix_values": centred(splits[8], (KVH, PREFIX, HD), 1.0, 6.0, ((1, 16),)),
        "prefix_segments": jnp.searchsorted(jnp.cumsum(uneven_parts(splits[9], NTRAJ, PREFIX, 2 * PREFIX // NTRAJ, 1)), jnp.arange(PREFIX), side="right").astype(jnp.int32),
        "stretch_segments": jnp.searchsorted(jnp.cumsum(uneven_parts(splits[10], NTRAJ, STRETCH, 2 * STRETCH // NTRAJ, 1)), jnp.arange(STRETCH), side="right").astype(jnp.int32),
        "stretch_offset": jax.random.randint(splits[11], (1,), PREFIX, 2 * PREFIX).astype(jnp.int32),
    }


ROPE_BASE = 500000.0
ROPE_FACTOR = 8.0
LOW_FREQ = 1.0
HIGH_FREQ = 4.0
INITIAL_SPAN = 8192.0
NORM_EPSILON = 1e-05
MASKED = -1e+30

def inverse_freqs(head_width):
    pair_index = jnp.arange(head_width // 2, dtype=jnp.float32)
    base_freq = ROPE_BASE ** (-2.0 * pair_index / head_width)
    wavelength = 2.0 * math.pi / base_freq
    smooth = (INITIAL_SPAN / wavelength - LOW_FREQ) / (HIGH_FREQ - LOW_FREQ)
    blended = (1.0 - smooth) * base_freq / ROPE_FACTOR + smooth * base_freq
    return jnp.where(wavelength < INITIAL_SPAN / HIGH_FREQ, base_freq, jnp.where(wavelength > INITIAL_SPAN / LOW_FREQ, base_freq / ROPE_FACTOR, blended))

def rotate(vectors, positions):
    head_width = vectors.shape[-1]
    angles = positions[..., None] * inverse_freqs(head_width)
    cosine = jnp.cos(angles)
    sinus = jnp.sin(angles)
    first_half = vectors[..., :head_width // 2]
    second_half = vectors[..., head_width // 2:]
    return jnp.concatenate([first_half * cosine - second_half * sinus, second_half * cosine + first_half * sinus], axis=-1)

def reference(stream, pending, norm_gain, w_query, w_key, w_value, w_out, prefix_keys, prefix_values, prefix_segments, stretch_segments, stretch_offset):
    stream_wide = stream.astype(jnp.float32)
    mean_square = lax.optimization_barrier(jnp.mean(stream_wide * stream_wide, axis=1, keepdims=True))
    normed = (stream_wide * lax.rsqrt(mean_square + NORM_EPSILON) * norm_gain.astype(jnp.float32)).astype(jnp.bfloat16)
    positions = stretch_offset[0].astype(jnp.float32) + jnp.arange(STRETCH, dtype=jnp.float32)
    queries = jnp.dot(normed, w_query, preferred_element_type=jnp.float32).reshape(STRETCH, HQ, HD)
    queries = rotate(queries, positions[:, None]).astype(jnp.bfloat16)
    new_keys = jnp.dot(normed, w_key, preferred_element_type=jnp.float32).reshape(STRETCH, KVH, HD)
    new_keys = rotate(new_keys, positions[:, None]).astype(jnp.bfloat16)
    new_values = jnp.dot(normed, w_value, preferred_element_type=jnp.float32).astype(jnp.bfloat16).reshape(STRETCH, KVH, HD)
    all_keys = jnp.concatenate([prefix_keys, jnp.transpose(new_keys, (1, 0, 2))], axis=1)
    all_values = jnp.concatenate([prefix_values, jnp.transpose(new_values, (1, 0, 2))], axis=1)
    stretch_index = jnp.arange(STRETCH, dtype=jnp.int32)
    earlier = prefix_segments[None, :] <= stretch_segments[:, None]
    same = (stretch_segments[None, :] == stretch_segments[:, None]) & (stretch_index[None, :] <= stretch_index[:, None])
    visible = jnp.concatenate([earlier, same], axis=1)
    group_size = HQ // KVH
    score_scale = 1.0 / math.sqrt(HD)

    def one_head(head_index):
        head_queries = lax.dynamic_index_in_dim(queries, head_index, axis=1, keepdims=False)
        kv_index = head_index // group_size
        head_keys = lax.dynamic_index_in_dim(all_keys, kv_index, axis=0, keepdims=False)
        head_values = lax.dynamic_index_in_dim(all_values, kv_index, axis=0, keepdims=False)
        scores = jnp.dot(head_queries, head_keys.T, preferred_element_type=jnp.float32) * score_scale
        scores = jnp.where(visible, scores, MASKED)
        row_max = lax.optimization_barrier(jnp.max(scores, axis=1, keepdims=True))
        weights = jnp.where(visible, jnp.exp(scores - row_max), 0.0)
        totals = lax.optimization_barrier(jnp.sum(weights, axis=1, keepdims=True))
        mixed = jnp.dot(weights.astype(jnp.bfloat16), head_values, preferred_element_type=jnp.float32)
        return (mixed / totals).astype(jnp.bfloat16)
    heads_out = lax.map(one_head, jnp.arange(HQ, dtype=jnp.int32))
    attended = jnp.transpose(heads_out, (1, 0, 2)).reshape(STRETCH, HQ * HD)
    group_cols = HQ * HD // N_TP

    def add_group(total, group_index):
        start = (group_index * group_cols).astype(jnp.int32)
        cols = lax.dynamic_slice_in_dim(attended, start, group_cols, 1)
        rows = lax.dynamic_slice_in_dim(w_out, start, group_cols, 0)
        part_low = lax.optimization_barrier(jnp.dot(cols, rows, preferred_element_type=jnp.float32).astype(jnp.bfloat16))
        return (total + part_low.astype(jnp.float32), None)
    head_sum, _ = lax.scan(add_group, jnp.zeros((STRETCH, D), jnp.float32), jnp.arange(N_TP, dtype=jnp.int32))
    carried = lax.optimization_barrier(jnp.sum(pending.astype(jnp.float32), axis=0))
    return (stream_wide + (head_sum + carried)).astype(jnp.bfloat16)
```

```python
import functools
import math

import jax
import jax.numpy as jnp
from jax import lax
from jax.experimental import pallas as pl
from jax.experimental.pallas import tpu as pltpu
from jax.sharding import PartitionSpec as P

MESH = pl.DeviceIdType.MESH
HD = 128
ROPE_BASE = 500000.0
ROPE_FACTOR = 8.0
LOW_FREQ = 1.0
HIGH_FREQ = 4.0
INITIAL_SPAN = 8192.0
NORM_EPSILON = 1e-05
MASKED = -1e30
LABEL_ROWS = 16


def inverse_freqs(head_width):
    pair_index = jnp.arange(head_width // 2, dtype=jnp.float32)
    base_freq = ROPE_BASE ** (-2.0 * pair_index / head_width)
    wavelength = 2.0 * math.pi / base_freq
    smooth = (INITIAL_SPAN / wavelength - LOW_FREQ) / (HIGH_FREQ - LOW_FREQ)
    blended = (1.0 - smooth) * base_freq / ROPE_FACTOR + smooth * base_freq
    return jnp.where(
        wavelength < INITIAL_SPAN / HIGH_FREQ,
        base_freq,
        jnp.where(wavelength > INITIAL_SPAN / LOW_FREQ, base_freq / ROPE_FACTOR, blended),
    )


def coords():
    c = lax.axis_index("ctx")
    t = lax.axis_index("tp")
    return c // 4, (c // 2) % 2, c % 2, t // 2, t % 2


def ctx_of(y, xh, core):
    return (y * 2 + xh) * 2 + core


def tp_of(z, xl):
    return z * 2 + xl


def neighbours():
    y, xh, core, z, xl = coords()
    here = ctx_of(y, xh, core)
    mine = tp_of(z, xl)
    return {
        "z+": (here, tp_of((z + 1) % 8, xl)),
        "z-": (here, tp_of((z + 7) % 8, xl)),
        "xl": (here, tp_of(z, 1 - xl)),
        "y+": (ctx_of((y + 1) % 4, xh, core), mine),
        "y-": (ctx_of((y + 3) % 4, xh, core), mine),
        "xh": (ctx_of(y, 1 - xh, core), mine),
        "xd": (ctx_of(y, 1 - xh, core), tp_of(z, 1 - xl)),
        "sib": (ctx_of(y, xh, 1 - core), mine),
    }


def greet(devices):
    barrier = pltpu.get_barrier_semaphore()
    for device in devices:
        pl.semaphore_signal(barrier, inc=1, device_id=device, device_id_type=MESH)
    pl.semaphore_wait(barrier, len(devices))


class Net:
    def __init__(self, links, send_sem, recv_sem):
        self.links, self.send_sem, self.recv_sem = links, send_sem, recv_sem
        self.copies = []

    def push(self, src, link, dst=None):
        k = len(self.copies)
        copy = pltpu.make_async_remote_copy(
            src_ref=src,
            dst_ref=src if dst is None else dst,
            send_sem=self.send_sem.at[k],
            recv_sem=self.recv_sem.at[k],
            device_id=self.links[link] if isinstance(link, str) else link,
            device_id_type=MESH,
        )
        copy.start()
        self.copies.append(copy)
        return copy

    def drain(self):
        for copy in self.copies:
            copy.wait_send()


class TpRing:
    def __init__(self, net, own, buf):
        self.net, self.buf = net, buf
        rows = own.shape[0]
        half, quarter = rows // 2, rows // 4
        self.low, self.high = pl.ds(0, half), pl.ds(half, half)
        self.parts = (pl.ds(half, quarter), pl.ds(half + quarter, quarter))
        _, _, _, z, xl = coords()
        t = tp_of(z, xl)
        self.swap = net.push(own.at[self.low], "xl", buf.at[t, self.low])
        self.hop = {}
        for way in ("z+", "z-"):
            self.hop[way, "own"] = net.push(own.at[self.low], way, buf.at[t, self.low])
            self.hop[way, "high"] = net.push(own.at[self.high], way, buf.at[t, self.high])
        self.across = [net.push(own.at[self.high], "xl", buf.at[t, self.high])]

    def cross(self):
        _, _, _, z, xl = coords()
        self.swap.wait_recv()
        for way in ("z+", "z-"):
            self.hop[way, "other"] = self.net.push(self.buf.at[tp_of(z, 1 - xl), self.low], way)

    def step(self, step):
        _, _, _, z, xl = coords()
        push, buf, hop = self.net.push, self.buf, self.hop
        for way, sign in (("z+", -1), ("z-", 1)):
            at = (z + sign * step + 8) % 8
            mine, theirs = tp_of(at, xl), tp_of(at, 1 - xl)
            part = 0 if way == "z+" else 1
            if step < 4:
                hop[way, "own"].wait_recv()
                if step < 3 or part == 0:
                    hop[way, "own"] = push(buf.at[mine, self.low], way)
                hop[way, "high"].wait_recv()
                rows = self.high if step < 3 else self.parts[part]
                hop[way, "high"] = push(buf.at[mine, rows], way)
                self.across.append(push(buf.at[mine, self.high], "xl"))
                hop[way, "other"].wait_recv()
                if step < 3 or part == 1:
                    hop[way, "other"] = push(buf.at[theirs, self.low], way)
            else:
                hop[way, "own" if part == 0 else "other"].wait_recv()
                hop[way, "high"].wait_recv()
                self.across.append(push(buf.at[mine, self.parts[part]], "xl"))

    def finish(self):
        for copy in self.across:
            copy.wait_recv()


class CtxRing:
    def __init__(self, net, own, buf, side_link):
        self.net, self.own, self.buf = net, own, buf
        y, xh, core, _, _ = coords()
        self.c, self.beside = ctx_of(y, xh, core), ctx_of(y, 1 - xh, core)
        self.side = net.push(own, side_link, buf.at[self.c])
        self.sib = [net.push(own, "sib", buf.at[self.c])]
        self.hop = {}

    def send_own(self):
        for way in ("y+", "y-"):
            self.hop[way, "own"] = self.net.push(self.own, way, self.buf.at[self.c])

    def send_side(self):
        self.side.wait_recv()
        for way in ("y+", "y-"):
            self.hop[way, "side"] = self.net.push(self.buf.at[self.beside], way)
        self.sib.append(self.net.push(self.buf.at[self.beside], "sib"))

    def step(self, step):
        y, xh, core, _, _ = coords()
        push, buf, hop = self.net.push, self.buf, self.hop
        for way, sign in (("y+", -1), ("y-", 1)):
            at = (y + sign * step + 4) % 4
            own, beside = ctx_of(at, xh, core), ctx_of(at, 1 - xh, core)
            first = way == "y+"
            if step == 1:
                hop[way, "own"].wait_recv()
                if first:
                    hop[way, "own"] = push(buf.at[own], way)
                self.sib.append(push(buf.at[own], "sib"))
                hop[way, "side"].wait_recv()
                if not first:
                    hop[way, "side"] = push(buf.at[beside], way)
                self.sib.append(push(buf.at[beside], "sib"))
            else:
                hop[way, "own" if first else "side"].wait_recv()
                self.sib.append(push(buf.at[own if first else beside], "sib"))

    def finish(self):
        for copy in self.sib:
            copy.wait_recv()


FRONT_COPIES = 96


def front_kernel(
    stream, weight, old, w_out, gain, cosine, sinus,
    query, cache, fresh, out_rows,
    blocks, weights, totals, squares, made, turned,
    local_sem, send_sem, recv_sem, turn_sem,
):
    y, xh, core, z, xl = coords()
    c, t = ctx_of(y, xh, core), tp_of(z, xl)
    links = neighbours()
    later = {}
    for ahead in (1, 2):
        for other in (0, 1):
            later[ahead, other] = ((c + ahead) % 16, tp_of(z, (xl + other) % 2))
    earlier = [
        ((c + 16 - ahead) % 16, tp_of(z, (xl + other) % 2)) for ahead in (1, 2) for other in (0, 1)
    ]
    barrier = pltpu.get_barrier_semaphore()

    @pl.when(c != t)
    def _():
        pl.semaphore_signal(barrier, inc=1, device_id=(t, c), device_id_type=MESH)

    local = [
        pltpu.make_async_copy(stream, blocks.at[t], local_sem.at[0]),
        pltpu.make_async_copy(weight, weights.at[c], local_sem.at[1]),
        pltpu.make_async_copy(old, cache.at[c], local_sem.at[2]),
    ]
    peers = list(links.values()) + list(later.values()) + earlier
    for device in peers:
        pl.semaphore_signal(barrier, inc=1, device_id=device, device_id_type=MESH)

    @pl.when(c != t)
    def _():
        pl.semaphore_wait(barrier, len(peers) + 1)

    @pl.when(c == t)
    def _():
        pl.semaphore_wait(barrier, len(peers))

    net = Net(links, send_sem, recv_sem)
    tp_ring = TpRing(net, stream, blocks)
    w_ring = CtxRing(net, weight, weights, "xh")
    w_ring.send_own()
    old_ring = CtxRing(net, old, cache, "xd")
    for copy in local:
        copy.start()
    turn = pltpu.make_async_remote_copy(
        src_ref=w_out,
        dst_ref=turned,
        send_sem=turn_sem.at[0],
        recv_sem=turn_sem.at[1],
        device_id=(t, c),
        device_id_type=MESH,
    )
    stay = pltpu.make_async_copy(w_out, turned, turn_sem.at[2])

    @pl.when(c != t)
    def _():
        turn.start()

    @pl.when(c == t)
    def _():
        stay.start()

    tp_ring.cross()
    w_ring.send_side()
    tp_ring.step(1)
    w_ring.step(1)
    old_ring.send_own()
    old_ring.send_side()
    tp_ring.step(2)
    w_ring.step(2)
    tp_ring.step(3)
    old_ring.step(1)

    @pl.when(c != t)
    def _():
        turn.wait_send()
        turn.wait_recv()

    @pl.when(c == t)
    def _():
        stay.wait()

    out_ring = CtxRing(net, turned, out_rows, "xh")
    out_ring.send_own()
    out_ring.send_side()
    own_out = pltpu.make_async_copy(turned, out_rows.at[c], local_sem.at[3])
    own_out.start()
    tp_ring.step(4)
    old_ring.step(2)
    w_ring.finish()
    tp_ring.finish()
    local[0].wait()
    local[1].wait()

    totals[...] = jnp.zeros_like(totals)
    squares[...] = jnp.zeros_like(squares)

    def project(b, _):
        wide = blocks[b].astype(jnp.float32)
        part = wide * wide
        squares[...] += sum(part[:, k * HD : (k + 1) * HD] for k in range(part.shape[1] // HD))
        low = (wide * gain[b]).astype(jnp.bfloat16)
        totals[...] += jnp.dot(low, weights[b], preferred_element_type=jnp.float32)
        return 0

    lax.fori_loop(0, 16, project, 0)
    width = 16 * stream.shape[1]
    mean_square = jnp.sum(squares[...], axis=1, keepdims=True) / width
    scale = lax.rsqrt(mean_square + NORM_EPSILON)
    cos, sin = cosine[...], sinus[...]

    def rotate(part):
        return part * cos + pltpu.roll(part, HD // 2, 1) * sin

    to_exponent = math.log2(math.e) / math.sqrt(HD)
    for h in range(2):
        part = totals[:, h * HD : (h + 1) * HD] * scale
        query[h] = (rotate(part) * to_exponent).astype(jnp.bfloat16)
    part = totals[:, 2 * HD :] * scale

    @pl.when(xl == 0)
    def _():
        made[...] = rotate(part).astype(jnp.bfloat16)

    @pl.when(xl == 1)
    def _():
        made[...] = part.astype(jnp.bfloat16)

    keep = pltpu.make_async_copy(made, fresh.at[xl, 2], local_sem.at[4])
    keep.start()
    sent = [net.push(made, "xl", fresh.at[xl, 2])]
    for (ahead, _), device in later.items():
        sent.append(net.push(made, device, fresh.at[xl, 2 - ahead]))

    old_ring.finish()
    out_ring.step(1)
    out_ring.step(2)
    out_ring.finish()
    for copy in sent:
        copy.wait_recv()
    keep.wait()
    local[2].wait()
    own_out.wait()
    net.drain()
    assert len(net.copies) <= FRONT_COPIES


def front(stream, weight, old, w_out, gain, cosine, sinus):
    rows, cols = stream.shape
    low = jnp.bfloat16
    any_spec = pl.BlockSpec(memory_space=pl.ANY)
    vmem = pl.BlockSpec(memory_space=pltpu.VMEM)
    return pl.pallas_call(
        front_kernel,
        out_shape=(
            jax.ShapeDtypeStruct((2, rows, HD), low),
            jax.ShapeDtypeStruct((16, *old.shape), low),
            jax.ShapeDtypeStruct((2, 3, rows, HD), low),
            jax.ShapeDtypeStruct((16, *w_out.shape), low),
        ),
        in_specs=[any_spec] * 4 + [vmem] * 3,
        out_specs=[vmem] + [any_spec] * 3,
        scratch_shapes=[
            pltpu.VMEM((16, rows, cols), low),
            pltpu.VMEM((16, *weight.shape), low),
            pltpu.VMEM((rows, weight.shape[1]), jnp.float32),
            pltpu.VMEM((rows, HD), jnp.float32),
            pltpu.VMEM((rows, HD), low),
            pltpu.VMEM(w_out.shape, low),
            pltpu.SemaphoreType.DMA((5,)),
            pltpu.SemaphoreType.DMA((FRONT_COPIES,)),
            pltpu.SemaphoreType.DMA((FRONT_COPIES,)),
            pltpu.SemaphoreType.DMA((3,)),
        ],
        compiler_params=pltpu.CompilerParams(
            collective_id=0, has_side_effects=True, vmem_limit_bytes=40 << 20
        ),
        name="front",
    )(stream, weight, old, w_out, gain, cosine, sinus)


def attend_kernel(query, fresh, marks, q_marks, old, result, top, total, mix):
    step = pl.program_id(0)
    c = lax.axis_index("ctx")
    heads, rows, _ = query.shape
    span = (old.shape[1] - LABEL_ROWS) // 2

    @pl.when(step == 0)
    def _():
        top[...] = jnp.full_like(top, MASKED)
        total[...] = jnp.zeros_like(total)
        mix[...] = jnp.zeros_like(mix)

    def absorb(h, keys, values, seen):
        scores = lax.dot_general(
            query[h], keys, (((1,), (1,)), ((), ())), preferred_element_type=jnp.float32
        )
        scores = jnp.where(seen, scores, MASKED)
        before = top[h]
        now = jnp.maximum(before, jnp.max(scores, axis=1, keepdims=True))
        fade = jnp.exp2(before - now)
        weights = jnp.exp2(scores - now[:, :1])
        total[h] = total[h] * fade + jnp.sum(weights, axis=1, keepdims=True)
        mix[h] = mix[h] * fade + jnp.dot(
            weights.astype(jnp.bfloat16), values, preferred_element_type=jnp.float32
        )
        top[h] = now

    def row_of(labels, count):
        wide = labels.astype(jnp.float32)
        return jnp.concatenate([wide[k : k + 1] for k in range(count)], axis=1)

    own = q_marks[...]
    prefix_marks = row_of(old[0, 2 * span :], span // HD)
    seen = prefix_marks <= own
    for h in range(heads):
        absorb(h, old[0, :span], old[0, span : 2 * span], seen)

    @pl.when(step == pl.num_programs(0) - 1)
    def _():
        first = span // HD
        for j in range(3):
            back = 2 - j
            labels = marks[(c + 16 - back) % 16].astype(jnp.float32)
            row = jnp.concatenate(
                [labels[first + k : first + k + 1] for k in range(rows // HD)], axis=1
            )
            row = jnp.where(c >= back, row, -1.0)
            same = row == own
            if back == 0:
                at = lax.broadcasted_iota(jnp.int32, (rows, rows), 0)
                key_at = lax.broadcasted_iota(jnp.int32, (rows, rows), 1)
                same = same & (key_at <= at)
            for h in range(heads):
                absorb(h, fresh[0, j], fresh[1, j], same)
        for h in range(heads):
            result[:, h * HD : (h + 1) * HD] = (mix[h] / total[h]).astype(jnp.bfloat16)


def attend(query, fresh, q_marks, cache):
    heads, rows, _ = query.shape
    span = cache.shape[1]
    return pl.pallas_call(
        attend_kernel,
        grid=(16,),
        out_shape=jax.ShapeDtypeStruct((rows, heads * HD), jnp.bfloat16),
        in_specs=[
            pl.BlockSpec(query.shape, lambda i: (0, 0, 0)),
            pl.BlockSpec(fresh.shape, lambda i: (0, 0, 0, 0)),
            pl.BlockSpec((16, LABEL_ROWS, HD), lambda i: (0, span // LABEL_ROWS - 1, 0)),
            pl.BlockSpec((rows, 1), lambda i: (0, 0)),
            pl.BlockSpec((1, span, HD), lambda i: (i, 0, 0)),
        ],
        out_specs=pl.BlockSpec((rows, heads * HD), lambda i: (0, 0)),
        scratch_shapes=[pltpu.VMEM((heads, rows, HD), jnp.float32) for _ in range(3)],
        compiler_params=pltpu.CompilerParams(vmem_limit_bytes=40 << 20),
        cost_estimate=pl.CostEstimate(
            flops=4 * heads * rows * 13440 * HD, bytes_accessed=7 << 20, transcendentals=heads * rows * 13440
        ),
        name="attend",
    )(query, fresh, cache, q_marks, cache)


BACK_COPIES = 40


def back_kernel(attended, out_rows, block, gathered, rows_here, local_sem, send_sem, recv_sem):
    _, _, _, z, xl = coords()
    t = tp_of(z, xl)
    links = neighbours()
    load = pltpu.make_async_copy(out_rows, rows_here, local_sem.at[0])
    load.start()
    gathered[t] = attended[...]
    greet([links[name] for name in ("z+", "z-", "xl")])
    net = Net(links, send_sem, recv_sem)
    ring = TpRing(net, attended, gathered)
    ring.cross()
    for step in (1, 2, 3, 4):
        ring.step(step)
    ring.finish()
    load.wait()
    block[...] = jnp.zeros_like(block)

    def add(b, _):
        block[...] += jnp.dot(gathered[b], rows_here[b], preferred_element_type=jnp.float32)
        return 0

    lax.fori_loop(0, 16, add, 0)
    net.drain()
    assert len(net.copies) <= BACK_COPIES


def back(attended, out_rows):
    rows, cols = attended.shape
    vmem = pl.BlockSpec(memory_space=pltpu.VMEM)
    return pl.pallas_call(
        back_kernel,
        out_shape=jax.ShapeDtypeStruct((rows, out_rows.shape[2]), jnp.float32),
        in_specs=[vmem, pl.BlockSpec(memory_space=pl.ANY)],
        out_specs=vmem,
        scratch_shapes=[
            pltpu.VMEM((16, rows, cols), jnp.bfloat16),
            pltpu.VMEM(out_rows.shape, jnp.bfloat16),
            pltpu.SemaphoreType.DMA((1,)),
            pltpu.SemaphoreType.DMA((BACK_COPIES,)),
            pltpu.SemaphoreType.DMA((BACK_COPIES,)),
        ],
        compiler_params=pltpu.CompilerParams(
            collective_id=1, has_side_effects=True, vmem_limit_bytes=30 << 20
        ),
        name="back",
    )(attended, out_rows)


def per_device(
    stream,
    pending,
    norm_gain,
    w_query,
    w_key,
    w_value,
    w_out,
    prefix_keys,
    prefix_values,
    prefix_segments,
    stretch_segments,
    stretch_offset,
):
    rows, cols = stream.shape
    z, xl = lax.axis_index("tp") // 2, lax.axis_index("tp") % 2
    carried = lax.psum_scatter(pending[0], "tp", scatter_dimension=1, tiled=True)

    token = lax.axis_index("ctx") * rows + jnp.arange(rows, dtype=jnp.int32)
    positions = stretch_offset[0].astype(jnp.float32) + token.astype(jnp.float32)
    angles = positions[:, None] * inverse_freqs(HD)
    cos, sin = jnp.cos(angles), jnp.sin(angles)
    cosine = jnp.concatenate([cos, cos], axis=1)
    sinus = jnp.concatenate([-sin, sin], axis=1)

    key_cols = lax.dynamic_slice_in_dim(w_key, z * HD, HD, 1)
    value_cols = lax.dynamic_slice_in_dim(w_value, z * HD, HD, 1)
    weight = jnp.concatenate([w_query, jnp.where(xl == 0, key_cols, value_cols)], axis=1)
    labels = jnp.concatenate([prefix_segments, stretch_segments]).reshape(-1, HD)
    labels = jnp.pad(labels, ((0, LABEL_ROWS - labels.shape[0]), (0, 0))).astype(jnp.bfloat16)
    old = jnp.concatenate(
        [
            lax.dynamic_index_in_dim(prefix_keys, z, 0, keepdims=False),
            lax.dynamic_index_in_dim(prefix_values, z, 0, keepdims=False),
            labels,
        ]
    )
    gain = norm_gain.astype(jnp.float32).reshape(16, 1, cols)
    query, cache, fresh, out_rows = front(stream, weight, old, w_out, gain, cosine, sinus)
    q_marks = stretch_segments.astype(jnp.float32)[:, None]
    attended = attend(query, fresh, q_marks, cache)
    heads = back(attended, out_rows)
    return (stream.astype(jnp.float32) + (heads + carried.astype(jnp.float32))).astype(jnp.bfloat16)


def solution(mesh):
    in_specs = (
        P("ctx", "tp"),
        P("tp", "ctx", None),
        P(),
        P("ctx", "tp"),
        P("ctx", None),
        P("ctx", None),
        P("tp", "ctx"),
        P(None, "ctx", None),
        P(None, "ctx", None),
        P("ctx"),
        P("ctx"),
        P(),
    )
    return jax.shard_map(
        per_device, mesh=mesh, in_specs=in_specs, out_specs=P("ctx", "tp"), check_vma=False
    )
```

```python
import functools
import math

import jax
import jax.numpy as jnp
from jax import lax
from jax.experimental import pallas as pl
from jax.experimental.pallas import tpu as pltpu
from jax.sharding import PartitionSpec as P

MESH = pl.DeviceIdType.MESH
HD = 128
ROPE_BASE = 500000.0
ROPE_FACTOR = 8.0
LOW_FREQ = 1.0
HIGH_FREQ = 4.0
INITIAL_SPAN = 8192.0
NORM_EPSILON = 1e-05
MASKED = -1e30
LABEL_ROWS = 16


def inverse_freqs(head_width):
    pair_index = jnp.arange(head_width // 2, dtype=jnp.float32)
    base_freq = ROPE_BASE ** (-2.0 * pair_index / head_width)
    wavelength = 2.0 * math.pi / base_freq
    smooth = (INITIAL_SPAN / wavelength - LOW_FREQ) / (HIGH_FREQ - LOW_FREQ)
    blended = (1.0 - smooth) * base_freq / ROPE_FACTOR + smooth * base_freq
    return jnp.where(
        wavelength < INITIAL_SPAN / HIGH_FREQ,
        base_freq,
        jnp.where(wavelength > INITIAL_SPAN / LOW_FREQ, base_freq / ROPE_FACTOR, blended),
    )


def coords():
    c = lax.axis_index("ctx")
    t = lax.axis_index("tp")
    return c // 4, (c // 2) % 2, c % 2, t // 2, t % 2


def ctx_of(y, xh, core):
    return (y * 2 + xh) * 2 + core


def tp_of(z, xl):
    return z * 2 + xl


def neighbours():
    y, xh, core, z, xl = coords()
    here = ctx_of(y, xh, core)
    mine = tp_of(z, xl)
    return {
        "z+": (here, tp_of((z + 1) % 8, xl)),
        "z-": (here, tp_of((z + 7) % 8, xl)),
        "xl": (here, tp_of(z, 1 - xl)),
        "y+": (ctx_of((y + 1) % 4, xh, core), mine),
        "y-": (ctx_of((y + 3) % 4, xh, core), mine),
        "xh": (ctx_of(y, 1 - xh, core), mine),
        "xd": (ctx_of(y, 1 - xh, core), tp_of(z, 1 - xl)),
        "sib": (ctx_of(y, xh, 1 - core), mine),
    }


def greet(devices):
    barrier = pltpu.get_barrier_semaphore()
    for device in devices:
        pl.semaphore_signal(barrier, inc=1, device_id=device, device_id_type=MESH)
    pl.semaphore_wait(barrier, len(devices))


class Copy:
    def __init__(self, net, k, ref, device):
        self.root, self.shape = getattr(ref, "ref", ref), ref.shape
        self.net, self.k, self.device = net, k, device

    def handle(self):
        lead = (0,) * (len(self.root.shape) - len(self.shape))
        like = self.root.at[(*lead, *(pl.ds(0, n) for n in self.shape))]
        return pltpu.make_async_remote_copy(
            src_ref=like,
            dst_ref=like,
            send_sem=self.net.send_sem.at[self.k],
            recv_sem=self.net.recv_sem.at[self.k],
            device_id=self.device,
            device_id_type=MESH,
        )

    def wait_recv(self):
        self.handle().wait_recv()

    def wait_send(self):
        self.handle().wait_send()


class Net:
    def __init__(self, links, send_sem, recv_sem):
        self.links, self.send_sem, self.recv_sem = links, send_sem, recv_sem
        self.copies = []

    def push(self, src, link, dst=None):
        k = len(self.copies)
        device = self.links[link] if isinstance(link, str) else link
        pltpu.make_async_remote_copy(
            src_ref=src,
            dst_ref=src if dst is None else dst,
            send_sem=self.send_sem.at[k],
            recv_sem=self.recv_sem.at[k],
            device_id=device,
            device_id_type=MESH,
        ).start()
        self.copies.append(Copy(self, k, src, device))
        return self.copies[-1]

    def drain(self):
        for copy in self.copies:
            copy.wait_send()


class TpRing:
    def __init__(self, net, own, buf):
        self.net, self.buf = net, buf
        rows = own.shape[0]
        half, quarter = rows // 2, rows // 4
        self.low, self.high = pl.ds(0, half), pl.ds(half, half)
        self.parts = (pl.ds(half, quarter), pl.ds(half + quarter, quarter))
        _, _, _, z, xl = coords()
        t = tp_of(z, xl)
        self.swap = net.push(own.at[self.low], "xl", buf.at[t, self.low])
        self.hop = {}
        for way in ("z+", "z-"):
            self.hop[way, "own"] = net.push(own.at[self.low], way, buf.at[t, self.low])
            self.hop[way, "high"] = net.push(own.at[self.high], way, buf.at[t, self.high])
        self.across = [net.push(own.at[self.high], "xl", buf.at[t, self.high])]

    def cross(self):
        _, _, _, z, xl = coords()
        self.swap.wait_recv()
        for way in ("z+", "z-"):
            self.hop[way, "other"] = self.net.push(self.buf.at[tp_of(z, 1 - xl), self.low], way)

    def step(self, step):
        _, _, _, z, xl = coords()
        push, buf, hop = self.net.push, self.buf, self.hop
        for way, sign in (("z+", -1), ("z-", 1)):
            at = (z + sign * step + 8) % 8
            mine, theirs = tp_of(at, xl), tp_of(at, 1 - xl)
            part = 0 if way == "z+" else 1
            if step < 4:
                hop[way, "own"].wait_recv()
                if step < 3 or part == 0:
                    hop[way, "own"] = push(buf.at[mine, self.low], way)
                hop[way, "high"].wait_recv()
                rows = self.high if step < 3 else self.parts[part]
                hop[way, "high"] = push(buf.at[mine, rows], way)
                self.across.append(push(buf.at[mine, self.high], "xl"))
                hop[way, "other"].wait_recv()
                if step < 3 or part == 1:
                    hop[way, "other"] = push(buf.at[theirs, self.low], way)
            else:
                hop[way, "own" if part == 0 else "other"].wait_recv()
                hop[way, "high"].wait_recv()
                self.across.append(push(buf.at[mine, self.parts[part]], "xl"))

    def finish(self):
        for copy in self.across:
            copy.wait_recv()


class CtxRing:
    def __init__(self, net, own, buf, side_link):
        self.net, self.own, self.buf = net, own, buf
        y, xh, core, _, _ = coords()
        self.c, self.beside = ctx_of(y, xh, core), ctx_of(y, 1 - xh, core)
        self.side = net.push(own, side_link, buf.at[self.c])
        self.sib = [net.push(own, "sib", buf.at[self.c])]
        self.hop = {}

    def send_own(self):
        for way in ("y+", "y-"):
            self.hop[way, "own"] = self.net.push(self.own, way, self.buf.at[self.c])

    def send_side(self):
        self.side.wait_recv()
        for way in ("y+", "y-"):
            self.hop[way, "side"] = self.net.push(self.buf.at[self.beside], way)
        self.sib.append(self.net.push(self.buf.at[self.beside], "sib"))

    def step(self, step):
        y, xh, core, _, _ = coords()
        push, buf, hop = self.net.push, self.buf, self.hop
        for way, sign in (("y+", -1), ("y-", 1)):
            at = (y + sign * step + 4) % 4
            own, beside = ctx_of(at, xh, core), ctx_of(at, 1 - xh, core)
            first = way == "y+"
            if step == 1:
                hop[way, "own"].wait_recv()
                if first:
                    hop[way, "own"] = push(buf.at[own], way)
                self.sib.append(push(buf.at[own], "sib"))
                hop[way, "side"].wait_recv()
                if not first:
                    hop[way, "side"] = push(buf.at[beside], way)
                self.sib.append(push(buf.at[beside], "sib"))
            else:
                hop[way, "own" if first else "side"].wait_recv()
                self.sib.append(push(buf.at[own if first else beside], "sib"))

    def finish(self):
        for copy in self.sib:
            copy.wait_recv()


class PendingSum:
    def __init__(self, net, pending, slabs, crossed, landed, landed_parts, final, sems):
        self.net, self.slabs, self.crossed = net, slabs, crossed
        self.landed, self.landed_parts, self.final = landed, landed_parts, final
        _, _, _, self.z, self.xl = coords()
        rows, cols = slabs.shape[1:]
        half, quarter = rows // 2, rows // 4
        self.low, self.high = pl.ds(0, half), pl.ds(half, half)
        self.parts = (pl.ds(half, quarter), pl.ds(half + quarter, quarter))
        self.loads = [
            pltpu.make_async_copy(
                pending.at[0, :, pl.ds(k * cols, cols)], slabs.at[k], sems.at[k]
            )
            for k in range(16)
        ]
        for load in self.loads:
            load.start()
        self.hop = {}

    def at(self, offset, other=0):
        return tp_of((self.z + offset + 8) % 8, (self.xl + other) % 2)

    def cross(self):
        for load in self.loads:
            load.wait()
        self.over = {}
        for offset in (4, 3, -3, 2, -2, 1, -1, 0):
            slot = (self.z + offset + 8) % 8
            self.over[offset] = self.net.push(
                self.slabs.at[self.at(offset, 1), self.high], "xl", self.crossed.at[slot]
            )

    def add(self, index, rows, more):
        total = self.slabs[index, rows].astype(jnp.float32) + more.astype(jnp.float32)
        self.slabs[index, rows] = total.astype(jnp.bfloat16)

    def take_crossed(self, offset):
        self.over[offset].wait_recv()
        slot = (self.z + offset + 8) % 8
        self.add(self.at(offset), self.high, self.crossed[slot])

    def land(self, way, kind, step):
        if kind == 2 and step == 0:
            return self.landed_parts.at[way]
        return self.landed.at[way, kind, step]

    def send(self, way, kind, step, index, rows):
        self.hop[way, kind] = self.net.push(
            self.slabs.at[index, rows], ("z+", "z-")[way], self.land(way, kind, step)
        )

    def first(self):
        self.send(0, 0, 0, self.at(4), self.low)
        self.send(1, 1, 0, self.at(4, 1), self.low)

    def first_high(self):
        self.take_crossed(4)
        for way in (0, 1):
            self.send(way, 2, 0, self.at(4), self.parts[way])

    def step(self, step):
        for way, sign in ((0, 1), (1, -1)):
            offset = sign * (4 - step)
            for kind in (0, 1, 2):
                index = self.at(offset, 1 if kind == 1 else 0)
                rows = self.high if kind == 2 else self.low
                if kind == 2:
                    self.take_crossed(offset)
                if step > 1 or kind == 2 or kind == way:
                    self.hop[way, kind].wait_recv()
                    into = self.parts[way] if kind == 2 and step == 1 else rows
                    self.add(index, into, self.land(way, kind, step - 1)[...])
                self.send(way, kind, step, index, rows)

    def last_other(self):
        for way in (0, 1):
            self.hop[way, 1].wait_recv()
        more = self.landed[0, 1, 3].astype(jnp.float32) + self.landed[1, 1, 3].astype(jnp.float32)
        self.add(self.at(0, 1), self.low, more)
        self.fold = self.net.push(self.slabs.at[self.at(0, 1), self.low], "xl", self.final)

    def last(self):
        wide = jnp.float32
        for way in (0, 1):
            self.hop[way, 0].wait_recv()
            self.hop[way, 2].wait_recv()
        self.over[0].wait_recv()
        self.fold.wait_recv()
        low = self.slabs[self.at(0), self.low].astype(wide) + self.final[...].astype(wide)
        low = low + self.landed[0, 0, 3].astype(wide) + self.landed[1, 0, 3].astype(wide)
        high = self.slabs[self.at(0), self.high].astype(wide) + self.crossed[self.z].astype(wide)
        high = high + self.landed[0, 2, 3].astype(wide) + self.landed[1, 2, 3].astype(wide)
        return low, high


COPIES = 208


def block_kernel(
    stream, pending, w_query, w_key, w_value, w_out, old_keys, old_values, labels,
    gain, cosine, sinus, q_marks,
    output,
    blocks, weights, cache, out_rows, gathered,
    slabs, crossed, landed, landed_parts, final,
    totals, squares, query, made, fresh, turned, attended, total_out,
    top, total, mix,
    local_sem, load_sem, send_sem, recv_sem, turn_sem,
):
    y, xh, core, z, xl = coords()
    c, t = ctx_of(y, xh, core), tp_of(z, xl)
    rows = stream.shape[0]
    span = old_keys.shape[1]
    q_cols = w_query.shape[1]
    heads = q_cols // HD

    local = [
        pltpu.make_async_copy(stream, blocks.at[t], local_sem.at[0]),
        pltpu.make_async_copy(w_query, weights.at[c, :, pl.ds(0, q_cols)], local_sem.at[1]),
        pltpu.make_async_copy(old_keys.at[z], cache.at[c, pl.ds(0, span)], local_sem.at[2]),
        pltpu.make_async_copy(old_values.at[z], cache.at[c, pl.ds(span, span)], local_sem.at[3]),
        pltpu.make_async_copy(labels, cache.at[c, pl.ds(2 * span, LABEL_ROWS)], local_sem.at[4]),
    ]
    head_cols = pl.ds(pl.multiple_of(z * HD, HD), HD)
    kv_slot = weights.at[c, :, pl.ds(q_cols, HD)]
    key_copy = pltpu.make_async_copy(w_key.at[:, head_cols], kv_slot, local_sem.at[5])
    value_copy = pltpu.make_async_copy(w_value.at[:, head_cols], kv_slot, local_sem.at[5])
    for copy in local:
        copy.start()

    @pl.when(xl == 0)
    def _():
        key_copy.start()

    @pl.when(xl == 1)
    def _():
        value_copy.start()

    links = neighbours()
    later = {}
    for ahead in (1, 2):
        for other in (0, 1):
            later[ahead, other] = ((c + ahead) % 16, tp_of(z, (xl + other) % 2))
    earlier = [
        ((c + 16 - ahead) % 16, tp_of(z, (xl + other) % 2)) for ahead in (1, 2) for other in (0, 1)
    ]
    peers = list(links.values()) + list(later.values()) + earlier
    barrier = pltpu.get_barrier_semaphore()
    for device in peers:
        pl.semaphore_signal(barrier, inc=1, device_id=device, device_id_type=MESH)

    @pl.when(c != t)
    def _():
        pl.semaphore_signal(barrier, inc=1, device_id=(t, c), device_id_type=MESH)
        pl.semaphore_wait(barrier, len(peers) + 1)

    @pl.when(c == t)
    def _():
        pl.semaphore_wait(barrier, len(peers))

    net = Net(links, send_sem, recv_sem)
    tp_ring = TpRing(net, stream, blocks)
    local[1].wait()
    key_copy.wait()
    w_ring = CtxRing(net, weights.at[c], weights, "xh")
    w_ring.send_own()
    for k in (2, 3, 4):
        local[k].wait()
    old_ring = CtxRing(net, cache.at[c], cache, "xd")

    turn = pltpu.make_async_remote_copy(
        src_ref=w_out,
        dst_ref=turned,
        send_sem=turn_sem.at[0],
        recv_sem=turn_sem.at[1],
        device_id=(t, c),
        device_id_type=MESH,
    )
    stay = pltpu.make_async_copy(w_out, turned, turn_sem.at[2])

    @pl.when(c != t)
    def _():
        turn.start()

    @pl.when(c == t)
    def _():
        stay.start()

    sums = PendingSum(net, pending, slabs, crossed, landed, landed_parts, final, load_sem)
    tp_ring.cross()
    w_ring.send_side()
    tp_ring.step(1)
    w_ring.step(1)
    old_ring.send_own()
    old_ring.send_side()
    tp_ring.step(2)
    w_ring.step(2)
    tp_ring.step(3)
    old_ring.step(1)

    @pl.when(c != t)
    def _():
        turn.wait_send()
        turn.wait_recv()

    @pl.when(c == t)
    def _():
        stay.wait()

    out_ring = CtxRing(net, turned, out_rows, "xh")
    out_ring.send_own()
    own_out = pltpu.make_async_copy(turned, out_rows.at[c], local_sem.at[6])
    own_out.start()
    tp_ring.step(4)
    sums.cross()
    sums.first()
    w_ring.finish()
    tp_ring.finish()
    local[0].wait()

    totals[...] = jnp.zeros_like(totals)
    squares[...] = jnp.zeros_like(squares)

    def project(b, _):
        wide = blocks[b].astype(jnp.float32)
        part = wide * wide
        squares[...] += sum(part[:, k * HD : (k + 1) * HD] for k in range(part.shape[1] // HD))
        low = (wide * gain[b]).astype(jnp.bfloat16)
        totals[...] += jnp.dot(low, weights[b], preferred_element_type=jnp.float32)
        return 0

    lax.fori_loop(0, 8, project, 0)
    sums.first_high()
    out_ring.send_side()
    lax.fori_loop(8, 16, project, 0)
    width = 16 * stream.shape[1]
    mean_square = jnp.sum(squares[...], axis=1, keepdims=True) / width
    scale = lax.rsqrt(mean_square + NORM_EPSILON)
    cos, sin = cosine[...], sinus[...]

    def rotate(part):
        return part * cos + pltpu.roll(part, HD // 2, 1) * sin

    part = totals[:, 2 * HD :] * scale

    @pl.when(xl == 0)
    def _():
        made[...] = rotate(part).astype(jnp.bfloat16)

    @pl.when(xl == 1)
    def _():
        made[...] = part.astype(jnp.bfloat16)

    keep = pltpu.make_async_copy(made, fresh.at[xl, 2], local_sem.at[7])
    keep.start()
    sent = [net.push(made, "xl", fresh.at[xl, 2])]
    for (ahead, _), device in later.items():
        sent.append(net.push(made, device, fresh.at[xl, 2 - ahead]))
    sums.step(1)

    to_exponent = math.log2(math.e) / math.sqrt(HD)
    for h in range(heads):
        part = totals[:, h * HD : (h + 1) * HD] * scale
        query[h] = (rotate(part) * to_exponent).astype(jnp.bfloat16)

    top[...] = jnp.full_like(top, MASKED)
    total[...] = jnp.zeros_like(total)
    mix[...] = jnp.zeros_like(mix)
    own_marks = q_marks[...]

    def absorb(h, keys, values, seen):
        scores = lax.dot_general(
            query[h], keys, (((1,), (1,)), ((), ())), preferred_element_type=jnp.float32
        )
        scores = jnp.where(seen, scores, MASKED)
        before = top[h]
        now = jnp.maximum(before, jnp.max(scores, axis=1, keepdims=True))
        fade = jnp.exp2(before - now)
        shares = jnp.exp2(scores - now[:, :1])
        total[h] = total[h] * fade + jnp.sum(shares, axis=1, keepdims=True)
        mix[h] = mix[h] * fade + jnp.dot(
            shares.astype(jnp.bfloat16), values, preferred_element_type=jnp.float32
        )
        top[h] = now

    def row_of(marks, first, count):
        wide = marks.astype(jnp.float32)
        return jnp.concatenate([wide[first + k : first + k + 1] for k in range(count)], axis=1)

    def over_prefix(i, _):
        def on(k, *actions):
            @pl.when(i == k)
            def _():
                for action in actions:
                    action()

        for k in range(16):
            if k in before_block:
                on(k, *before_block[k])
        group = i // 4
        turn_y = jnp.where(group == 1, 3, jnp.where(group == 2, 1, jnp.where(group == 3, 2, 0)))
        at = ctx_of((y + turn_y) % 4, (xh + (i // 2) % 2) % 2, (core + i % 2) % 2)
        marks = row_of(cache[at, 2 * span :], 0, span // HD)
        seen = marks <= own_marks
        for h in range(heads):
            absorb(h, cache[at, :span], cache[at, span : 2 * span], seen)
        return 0

    def sib(ring, *numbers):
        def wait():
            for k in numbers:
                ring.sib[k].wait_recv()

        return wait

    before_block = {
        0: [sib(old_ring, 0, 1)],
        2: [lambda: old_ring.step(2), lambda: out_ring.step(1)],
        4: [sib(old_ring, 2, 3)],
        6: [lambda: sums.step(2)],
        8: [sib(old_ring, 4, 5), lambda: out_ring.step(2)],
        12: [sib(old_ring, 6, 7)],
        13: [lambda: sums.step(3)],
    }
    lax.fori_loop(0, 16, over_prefix, 0)
    for copy in sent:
        copy.wait_recv()
    keep.wait()
    for j in range(3):
        back = 2 - j
        row = row_of(cache[(c + 16 - back) % 16, 2 * span :], span // HD, rows // HD)
        row = jnp.where(c >= back, row, -1.0)
        same = row == own_marks
        if back == 0:
            at = lax.broadcasted_iota(jnp.int32, (rows, rows), 0)
            key_at = lax.broadcasted_iota(jnp.int32, (rows, rows), 1)
            same = same & (key_at <= at)
        for h in range(heads):
            absorb(h, fresh[0, j], fresh[1, j], same)
    for h in range(heads):
        attended[:, h * HD : (h + 1) * HD] = (mix[h] / total[h]).astype(jnp.bfloat16)

    ring = TpRing(net, attended, gathered)
    gathered[t] = attended[...]
    sums.last_other()
    out_ring.finish()
    own_out.wait()
    ring.cross()
    for step in (1, 2, 3, 4):
        ring.step(step)
    low, high = sums.last()
    half = rows // 2
    total_out[:half] = low
    total_out[half:] = high
    ring.finish()

    def project_out(b, _):
        total_out[...] += jnp.dot(gathered[b], out_rows[b], preferred_element_type=jnp.float32)
        return 0

    lax.fori_loop(0, 16, project_out, 0)
    output[...] = (blocks[t].astype(jnp.float32) + total_out[...]).astype(jnp.bfloat16)
    net.drain()
    assert len(net.copies) <= COPIES


def run_block(stream, pending, w_query, w_key, w_value, w_out, old_keys, old_values, labels,
              gain, cosine, sinus, q_marks):
    rows, cols = stream.shape
    depth, q_cols = w_query.shape
    span = old_keys.shape[1]
    low, wide = jnp.bfloat16, jnp.float32
    half = rows // 2
    any_spec = pl.BlockSpec(memory_space=pl.ANY)
    vmem = pl.BlockSpec(memory_space=pltpu.VMEM)
    heads = q_cols // HD
    return pl.pallas_call(
        block_kernel,
        out_shape=jax.ShapeDtypeStruct((rows, cols), low),
        in_specs=[any_spec] * 9 + [vmem] * 4,
        out_specs=vmem,
        scratch_shapes=[
            pltpu.VMEM((16, rows, cols), low),
            pltpu.VMEM((16, depth, q_cols + HD), low),
            pltpu.VMEM((16, 2 * span + LABEL_ROWS, HD), low),
            pltpu.VMEM((16, *w_out.shape), low),
            pltpu.VMEM((16, rows, q_cols), low),
            pltpu.VMEM((16, rows, cols), low),
            pltpu.VMEM((8, half, cols), low),
            pltpu.VMEM((2, 3, 4, half, cols), low),
            pltpu.VMEM((2, half // 2, cols), low),
            pltpu.VMEM((half, cols), low),
            pltpu.VMEM((rows, q_cols + HD), wide),
            pltpu.VMEM((rows, HD), wide),
            pltpu.VMEM((heads, rows, HD), low),
            pltpu.VMEM((rows, HD), low),
            pltpu.VMEM((2, 3, rows, HD), low),
            pltpu.VMEM(w_out.shape, low),
            pltpu.VMEM((rows, q_cols), low),
            pltpu.VMEM((rows, cols), wide),
            pltpu.VMEM((heads, rows, HD), wide),
            pltpu.VMEM((heads, rows, HD), wide),
            pltpu.VMEM((heads, rows, HD), wide),
            pltpu.SemaphoreType.DMA((8,)),
            pltpu.SemaphoreType.DMA((16,)),
            pltpu.SemaphoreType.DMA((COPIES,)),
            pltpu.SemaphoreType.DMA((COPIES,)),
            pltpu.SemaphoreType.DMA((3,)),
        ],
        compiler_params=pltpu.CompilerParams(
            collective_id=0, has_side_effects=True, vmem_limit_bytes=58 << 20
        ),
        name="attention_block",
    )(stream, pending, w_query, w_key, w_value, w_out, old_keys, old_values, labels,
      gain, cosine, sinus, q_marks)


def per_device(
    stream,
    pending,
    norm_gain,
    w_query,
    w_key,
    w_value,
    w_out,
    prefix_keys,
    prefix_values,
    prefix_segments,
    stretch_segments,
    stretch_offset,
):
    rows, cols = stream.shape
    token = lax.axis_index("ctx") * rows + jnp.arange(rows, dtype=jnp.int32)
    positions = stretch_offset[0].astype(jnp.float32) + token.astype(jnp.float32)
    angles = positions[:, None] * inverse_freqs(HD)
    cos, sin = jnp.cos(angles), jnp.sin(angles)
    cosine = jnp.concatenate([cos, cos], axis=1)
    sinus = jnp.concatenate([-sin, sin], axis=1)
    labels = jnp.concatenate([prefix_segments, stretch_segments]).reshape(-1, HD)
    labels = jnp.pad(labels, ((0, LABEL_ROWS - labels.shape[0]), (0, 0))).astype(jnp.bfloat16)
    gain = norm_gain.astype(jnp.float32).reshape(16, 1, cols)
    q_marks = stretch_segments.astype(jnp.float32)[:, None]
    return run_block(
        stream, pending, w_query, w_key, w_value, w_out, prefix_keys, prefix_values, labels,
        gain, cosine, sinus, q_marks,
    )


def solution(mesh):
    in_specs = (
        P("ctx", "tp"),
        P("tp", "ctx", None),
        P(),
        P("ctx", "tp"),
        P("ctx", None),
        P("ctx", None),
        P("tp", "ctx"),
        P(None, "ctx", None),
        P(None, "ctx", None),
        P("ctx"),
        P("ctx"),
        P(),
    )
    return jax.shard_map(
        per_device, mesh=mesh, in_specs=in_specs, out_specs=P("ctx", "tp"), check_vma=False
    )
```

```python
import functools
import math

import jax
import jax.numpy as jnp
from jax import lax
from jax.experimental import pallas as pl
from jax.experimental.pallas import tpu as pltpu
from jax.sharding import PartitionSpec as P

MESH = pl.DeviceIdType.MESH
HD = 128
ROPE_BASE = 500000.0
ROPE_FACTOR = 8.0
LOW_FREQ = 1.0
HIGH_FREQ = 4.0
INITIAL_SPAN = 8192.0
NORM_EPSILON = 1e-05
MASKED = -1e30
LABEL_ROWS = 16


def inverse_freqs(head_width):
    pair_index = jnp.arange(head_width // 2, dtype=jnp.float32)
    base_freq = ROPE_BASE ** (-2.0 * pair_index / head_width)
    wavelength = 2.0 * math.pi / base_freq
    smooth = (INITIAL_SPAN / wavelength - LOW_FREQ) / (HIGH_FREQ - LOW_FREQ)
    blended = (1.0 - smooth) * base_freq / ROPE_FACTOR + smooth * base_freq
    return jnp.where(
        wavelength < INITIAL_SPAN / HIGH_FREQ,
        base_freq,
        jnp.where(wavelength > INITIAL_SPAN / LOW_FREQ, base_freq / ROPE_FACTOR, blended),
    )


def coords():
    c = lax.axis_index("ctx")
    t = lax.axis_index("tp")
    return c // 4, (c // 2) % 2, c % 2, t // 2, t % 2


def ctx_of(y, xh, core):
    return (y * 2 + xh) * 2 + core


def tp_of(z, xl):
    return z * 2 + xl


def neighbours():
    y, xh, core, z, xl = coords()
    here = ctx_of(y, xh, core)
    mine = tp_of(z, xl)
    return {
        "z+": (here, tp_of((z + 1) % 8, xl)),
        "z-": (here, tp_of((z + 7) % 8, xl)),
        "xl": (here, tp_of(z, 1 - xl)),
        "y+": (ctx_of((y + 1) % 4, xh, core), mine),
        "y-": (ctx_of((y + 3) % 4, xh, core), mine),
        "xh": (ctx_of(y, 1 - xh, core), mine),
        "xd": (ctx_of(y, 1 - xh, core), tp_of(z, 1 - xl)),
        "sib": (ctx_of(y, xh, 1 - core), mine),
    }


def greet(devices):
    barrier = pltpu.get_barrier_semaphore()
    for device in devices:
        pl.semaphore_signal(barrier, inc=1, device_id=device, device_id_type=MESH)
    pl.semaphore_wait(barrier, len(devices))


class Copy:
    def __init__(self, net, k, ref, device):
        self.root, self.shape = getattr(ref, "ref", ref), ref.shape
        self.net, self.k, self.device = net, k, device

    def handle(self):
        lead = (0,) * (len(self.root.shape) - len(self.shape))
        like = self.root.at[(*lead, *(pl.ds(0, n) for n in self.shape))]
        return pltpu.make_async_remote_copy(
            src_ref=like,
            dst_ref=like,
            send_sem=self.net.send_sem.at[self.k],
            recv_sem=self.net.recv_sem.at[self.k],
            device_id=self.device,
            device_id_type=MESH,
        )

    def wait_recv(self):
        self.handle().wait_recv()

    def wait_send(self):
        self.handle().wait_send()


class Net:
    def __init__(self, links, send_sem, recv_sem):
        self.links, self.send_sem, self.recv_sem = links, send_sem, recv_sem
        self.copies = []

    def push(self, src, link, dst=None):
        k = len(self.copies)
        device = self.links[link] if isinstance(link, str) else link
        pltpu.make_async_remote_copy(
            src_ref=src,
            dst_ref=src if dst is None else dst,
            send_sem=self.send_sem.at[k],
            recv_sem=self.recv_sem.at[k],
            device_id=device,
            device_id_type=MESH,
        ).start()
        self.copies.append(Copy(self, k, src, device))
        return self.copies[-1]

    def drain(self):
        for copy in self.copies:
            copy.wait_send()


class TpRing:
    def __init__(self, net, own, buf, upper):
        self.net, self.own, self.buf = net, own, buf
        half = own.shape[0] - upper
        part = -(-upper // 32) * 16
        self.low, self.high = pl.ds(0, half), pl.ds(half, upper)
        self.parts = (pl.ds(half, part), pl.ds(half + part, upper - part))
        _, _, _, z, xl = coords()
        t = tp_of(z, xl)
        self.swap = net.push(own.at[self.low], "xl", buf.at[t, self.low])
        self.hop = {}
        for way in ("z+", "z-"):
            self.hop[way, "own"] = net.push(own.at[self.low], way, buf.at[t, self.low])
            self.hop[way, "high"] = net.push(own.at[self.high], way, buf.at[t, self.high])
        self.across = []

    def cross(self):
        _, _, _, z, xl = coords()
        self.swap.wait_recv()
        for way in ("z+", "z-"):
            self.hop[way, "other"] = self.net.push(self.buf.at[tp_of(z, 1 - xl), self.low], way)
        self.across.append(
            self.net.push(self.own.at[self.high], "xl", self.buf.at[tp_of(z, xl), self.high])
        )

    def step(self, step):
        _, _, _, z, xl = coords()
        push, buf, hop = self.net.push, self.buf, self.hop
        for kind in ("own", "high", "other"):
            for way, sign in (("z+", -1), ("z-", 1)):
                at = (z + sign * step + 8) % 8
                mine, theirs = tp_of(at, xl), tp_of(at, 1 - xl)
                part = 0 if way == "z+" else 1
                if kind == "high":
                    hop[way, kind].wait_recv()
                    if step < 4:
                        rows = self.high if step < 3 else self.parts[part]
                        hop[way, kind] = push(buf.at[mine, rows], way)
                    rows = self.high if step < 4 else self.parts[part]
                    self.across.append(push(buf.at[mine, rows], "xl"))
                    continue
                last = part == (0 if kind == "own" else 1)
                if step < 4 or last:
                    hop[way, kind].wait_recv()
                if step < 3 or (step == 3 and last):
                    hop[way, kind] = push(buf.at[mine if kind == "own" else theirs, self.low], way)

    def arrive(self, first, last):
        for copy in self.across[first:last]:
            copy.wait_recv()


class CtxRing:
    def __init__(self, net, own, slot, side_link):
        self.net, self.own, self.slot, self.side_link = net, own, slot, side_link
        y, xh, core, _, _ = coords()
        self.c, self.beside = ctx_of(y, xh, core), ctx_of(y, 1 - xh, core)
        self.sib, self.hop = [], {}

    def send_across(self):
        self.side = self.net.push(self.own, self.side_link, self.slot(self.c))
        self.sib.append(self.net.push(self.own, "sib", self.slot(self.c)))

    def send_own(self):
        for way in ("y+", "y-"):
            self.hop[way, "own"] = self.net.push(self.own, way, self.slot(self.c))

    def send_side(self):
        self.side.wait_recv()
        for way in ("y+", "y-"):
            self.hop[way, "side"] = self.net.push(self.slot(self.beside), way)
        self.sib.append(self.net.push(self.slot(self.beside), "sib"))

    def came(self, way, step, kind):
        y, xh, core, _, _ = coords()
        at = (y + (-step if way == "y+" else step) + 4) % 4
        self.hop[way, kind].wait_recv()
        return self.slot(ctx_of(at, xh if kind == "own" else 1 - xh, core))

    def near(self, kind):
        for way in ("y+", "y-"):
            block = self.came(way, 1, kind)
            if (way == "y+") == (kind == "own"):
                self.hop[way, kind] = self.net.push(block, way)
            self.sib.append(self.net.push(block, "sib"))

    def far(self):
        for way, kind in (("y+", "own"), ("y-", "side")):
            self.sib.append(self.net.push(self.came(way, 2, kind), "sib"))

    def finish(self):
        for copy in self.sib:
            copy.wait_recv()


class Turn:
    def __init__(self, net, w_out, mid, turned, sems):
        self.net, self.w_out, self.mid, self.turned, self.sems = net, w_out, mid, turned, sems
        y, xh, core, z, xl = coords()
        self.eighth = y * 2 + xh
        self.rows = w_out.shape[0] // 8
        self.stays = core == xl

    def place(self, ahead):
        _, _, core, z, xl = coords()
        at = (self.eighth + ahead) % 8
        return (at * 2 + xl, tp_of(z, core))

    def height(self, ahead):
        _, _, _, z, xl = coords()
        c = lax.axis_index("ctx")
        return (c, tp_of((z + ahead) % 8, xl))

    def first(self):
        src = self.w_out.at[pl.ds(pl.multiple_of(self.eighth * self.rows, self.rows), self.rows)]
        dst = self.mid.at[self.eighth]
        away = pltpu.make_async_remote_copy(
            src_ref=src,
            dst_ref=dst,
            send_sem=self.sems.at[0],
            recv_sem=self.sems.at[1],
            device_id=self.place(0),
            device_id_type=MESH,
        )
        return away, pltpu.make_async_copy(src, dst, self.sems.at[2])

    def spread(self):
        away, stay = self.first()
        pl.when(jnp.logical_not(self.stays))(away.start)
        pl.when(self.stays)(stay.start)
        self.got = []
        for ahead in range(1, 8):
            at = (self.eighth + ahead) % 8
            src = self.w_out.at[pl.ds(pl.multiple_of(at * self.rows, self.rows), self.rows)]
            self.got.append(self.net.push(src, self.place(ahead), self.mid.at[self.eighth]))

    def own(self, z):
        core = lax.axis_index("ctx") % 2
        return self.turned.at[z, core, self.eighth]

    def rise(self):
        away, stay = self.first()

        @pl.when(jnp.logical_not(self.stays))
        def _():
            away.wait_send()
            away.wait_recv()

        pl.when(self.stays)(stay.wait)
        for copy in self.got:
            copy.wait_recv()
        _, _, _, z, _ = coords()
        keep = pltpu.make_async_copy(self.mid.at[z], self.own(z), self.sems.at[3])
        keep.start()
        self.risen = [
            self.net.push(self.mid.at[(z + ahead) % 8], self.height(ahead), self.own(z))
            for ahead in range(1, 8)
        ]

    def finish(self):
        _, _, _, z, _ = coords()
        pltpu.make_async_copy(self.mid.at[z], self.own(z), self.sems.at[3]).wait()
        for copy in self.risen:
            copy.wait_recv()


class PendingSum:
    def __init__(self, net, pending, slabs, crossed, landed, landed_parts, final, sems):
        self.net, self.slabs, self.crossed = net, slabs, crossed
        self.landed, self.landed_parts, self.final = landed, landed_parts, final
        _, _, _, self.z, self.xl = coords()
        rows, cols = slabs.shape[1:]
        half, quarter = rows // 2, rows // 4
        self.low, self.high = pl.ds(0, half), pl.ds(half, half)
        self.parts = (pl.ds(half, quarter), pl.ds(half + quarter, quarter))
        self.loads = [
            pltpu.make_async_copy(
                pending.at[0, :, pl.ds(k * cols, cols)], slabs.at[k], sems.at[k]
            )
            for k in range(16)
        ]
        for load in self.loads:
            load.start()
        self.hop, self.over = {}, {}

    def at(self, offset, other=0):
        return tp_of((self.z + offset + 8) % 8, (self.xl + other) % 2)

    def ready(self):
        for load in self.loads:
            load.wait()

    def cross(self, *offsets):
        for offset in offsets:
            slot = (self.z + offset + 8) % 8
            self.over[offset] = self.net.push(
                self.slabs.at[self.at(offset, 1), self.high], "xl", self.crossed.at[slot]
            )

    def add(self, index, rows, more):
        total = self.slabs[index, rows].astype(jnp.float32) + more.astype(jnp.float32)
        self.slabs[index, rows] = total.astype(jnp.bfloat16)

    def take_crossed(self, offset):
        self.over[offset].wait_recv()
        slot = (self.z + offset + 8) % 8
        self.add(self.at(offset), self.high, self.crossed[slot])

    def land(self, way, kind, step):
        if kind == 2 and step == 0:
            return self.landed_parts.at[way]
        return self.landed.at[way, kind, step]

    def send(self, way, kind, step, index, rows):
        self.hop[way, kind] = self.net.push(
            self.slabs.at[index, rows], ("z+", "z-")[way], self.land(way, kind, step)
        )

    def first(self):
        self.send(0, 0, 0, self.at(4), self.low)
        self.send(1, 1, 0, self.at(4, 1), self.low)

    def first_high(self):
        self.take_crossed(4)
        for way in (0, 1):
            self.send(way, 2, 0, self.at(4), self.parts[way])

    def step(self, step, kinds):
        for way, sign in ((0, 1), (1, -1)):
            offset = sign * (4 - step)
            for kind in kinds:
                index = self.at(offset, 1 if kind == 1 else 0)
                rows = self.high if kind == 2 else self.low
                if kind == 2:
                    self.take_crossed(offset)
                if step > 1 or kind == 2 or kind == way:
                    self.hop[way, kind].wait_recv()
                    into = self.parts[way] if kind == 2 and step == 1 else rows
                    self.add(index, into, self.land(way, kind, step - 1)[...])
                self.send(way, kind, step, index, rows)

    def last_other(self):
        for way in (0, 1):
            self.hop[way, 1].wait_recv()
        more = self.landed[0, 1, 3].astype(jnp.float32) + self.landed[1, 1, 3].astype(jnp.float32)
        self.add(self.at(0, 1), self.low, more)
        self.fold = self.net.push(self.slabs.at[self.at(0, 1), self.low], "xl", self.final)

    def last(self):
        wide = jnp.float32
        for way in (0, 1):
            self.hop[way, 0].wait_recv()
            self.hop[way, 2].wait_recv()
        self.over[0].wait_recv()
        self.fold.wait_recv()
        low = self.slabs[self.at(0), self.low].astype(wide) + self.final[...].astype(wide)
        low = low + self.landed[0, 0, 3].astype(wide) + self.landed[1, 0, 3].astype(wide)
        high = self.slabs[self.at(0), self.high].astype(wide) + self.crossed[self.z].astype(wide)
        high = high + self.landed[0, 2, 3].astype(wide) + self.landed[1, 2, 3].astype(wide)
        return low, high


COPIES = 256


def block_kernel(
    stream, pending, w_query, w_key, w_value, w_out, old_keys, old_values, labels,
    gain, cosine, sinus,
    output,
    blocks, weights, cache, out_rows, gathered,
    slabs, crossed, landed, landed_parts, final,
    totals, squares, query, made, fresh, mid, attended, total_out, q_marks,
    top, total, mix,
    local_sem, load_sem, send_sem, recv_sem, turn_sem,
):
    y, xh, core, z, xl = coords()
    c, t = ctx_of(y, xh, core), tp_of(z, xl)
    rows = stream.shape[0]
    span = old_keys.shape[1]
    q_cols = w_query.shape[1]
    heads = q_cols // HD

    def row_of(marks, first, count):
        wide = marks.astype(jnp.float32)
        return jnp.concatenate([wide[first + k : first + k + 1] for k in range(count)], axis=1)

    def arrival(j):
        away = (j + 2) // 4
        sign = 1 - 2 * (((j + 2) // 2) % 2)
        return tp_of((z + sign * away + 8) % 8, (xl + j % 2) % 2)

    local = [
        pltpu.make_async_copy(stream, blocks.at[t], local_sem.at[0]),
        pltpu.make_async_copy(w_query, weights.at[c, :, pl.ds(0, q_cols)], local_sem.at[1]),
        pltpu.make_async_copy(old_keys.at[z], cache.at[c, pl.ds(0, span)], local_sem.at[2]),
        pltpu.make_async_copy(old_values.at[z], cache.at[c, pl.ds(span, span)], local_sem.at[3]),
        pltpu.make_async_copy(labels, cache.at[c, pl.ds(2 * span, LABEL_ROWS)], local_sem.at[4]),
    ]
    head_cols = pl.ds(pl.multiple_of(z * HD, HD), HD)
    kv_slot = weights.at[c, :, pl.ds(q_cols, HD)]
    key_copy = pltpu.make_async_copy(w_key.at[:, head_cols], kv_slot, local_sem.at[5])
    value_copy = pltpu.make_async_copy(w_value.at[:, head_cols], kv_slot, local_sem.at[5])
    for copy in local:
        copy.start()

    @pl.when(xl == 0)
    def _():
        key_copy.start()

    @pl.when(xl == 1)
    def _():
        value_copy.start()

    links = neighbours()
    later = {}
    for ahead in (1, 2):
        for other in (0, 1):
            later[ahead, other] = ((c + ahead) % 16, tp_of(z, (xl + other) % 2))
    earlier = [
        ((c + 16 - ahead) % 16, tp_of(z, (xl + other) % 2)) for ahead in (1, 2) for other in (0, 1)
    ]
    net = Net(links, send_sem, recv_sem)
    turn = Turn(net, w_out, mid, out_rows, turn_sem)
    peers = list(links.values()) + list(later.values()) + earlier
    peers += [turn.place(ahead) for ahead in range(1, 8)]
    peers += [turn.height(ahead) for ahead in range(2, 7)]
    barrier = pltpu.get_barrier_semaphore()
    for device in peers:
        pl.semaphore_signal(barrier, inc=1, device_id=device, device_id_type=MESH)

    @pl.when(core != xl)
    def _():
        pl.semaphore_signal(barrier, inc=1, device_id=turn.place(0), device_id_type=MESH)
        pl.semaphore_wait(barrier, len(peers) + 1)

    @pl.when(core == xl)
    def _():
        pl.semaphore_wait(barrier, len(peers))

    tp_ring = TpRing(net, stream, blocks, 176)
    local[1].wait()
    key_copy.wait()
    w_ring = CtxRing(net, weights.at[c], lambda k: weights.at[k], "xh")
    w_ring.send_own()
    w_ring.send_across()
    for k in (2, 3, 4):
        local[k].wait()
    old_ring = CtxRing(net, cache.at[c], lambda k: cache.at[k], "xd")
    out_ring = CtxRing(
        net, turn.own(pl.ds(0, 8)), lambda k: out_rows.at[:, k % 2, k // 2], "xh"
    )
    sums = PendingSum(net, pending, slabs, crossed, landed, landed_parts, final, load_sem)
    row = row_of(cache[c, 2 * span :], span // HD, rows // HD)
    flat = (rows, rows)
    diagonal = lax.broadcasted_iota(jnp.int32, flat, 0) == lax.broadcasted_iota(jnp.int32, flat, 1)
    q_marks[...] = jnp.sum(jnp.where(diagonal, row, 0.0), axis=1, keepdims=True) + jnp.zeros(
        (rows, HD), jnp.float32
    )
    totals[...] = jnp.zeros_like(totals)
    squares[...] = jnp.zeros_like(squares)
    tp_ring.cross()
    turn.spread()
    w_ring.near("own")
    tp_ring.step(1)
    w_ring.send_side()
    old_ring.send_across()
    tp_ring.step(2)
    w_ring.near("side")
    w_ring.far()
    old_ring.send_own()
    old_ring.send_side()
    tp_ring.step(3)
    sums.ready()
    sums.cross(4)
    w_ring.finish()
    tp_ring.arrive(0, 5)
    local[0].wait()

    def project(j, _):
        b = arrival(j)
        wide = blocks[b].astype(jnp.float32)
        part = wide * wide
        squares[...] += sum(part[:, k * HD : (k + 1) * HD] for k in range(part.shape[1] // HD))
        low = (wide * gain[b]).astype(jnp.bfloat16)
        totals[...] += jnp.dot(low, weights[b], preferred_element_type=jnp.float32)
        return 0

    lax.fori_loop(0, 10, project, 0)
    tp_ring.step(4)
    sums.first()
    sums.first_high()
    turn.rise()
    old_ring.near("own")
    tp_ring.arrive(5, 9)
    sums.cross(3, -3)
    lax.fori_loop(10, 16, project, 0)
    width = 16 * stream.shape[1]
    mean_square = jnp.sum(squares[...], axis=1, keepdims=True) / width
    scale = lax.rsqrt(mean_square + NORM_EPSILON)
    cos = jnp.concatenate([cosine[...], cosine[...]], axis=1)
    sin = jnp.concatenate([-sinus[...], sinus[...]], axis=1)

    def rotate(part):
        return part * cos + pltpu.roll(part, HD // 2, 1) * sin

    part = totals[:, 2 * HD :] * scale

    @pl.when(xl == 0)
    def _():
        made[...] = rotate(part).astype(jnp.bfloat16)

    @pl.when(xl == 1)
    def _():
        made[...] = part.astype(jnp.bfloat16)

    keep = pltpu.make_async_copy(made, fresh.at[xl, 2], local_sem.at[7])
    keep.start()
    sent = [net.push(made, "xl", fresh.at[xl, 2])]
    for (ahead, _), device in later.items():
        sent.append(net.push(made, device, fresh.at[xl, 2 - ahead]))
    sums.step(1, (0, 1))

    to_exponent = math.log2(math.e) / math.sqrt(HD)
    for h in range(heads):
        part = totals[:, h * HD : (h + 1) * HD] * scale
        query[h] = (rotate(part) * to_exponent).astype(jnp.bfloat16)

    top[...] = jnp.full_like(top, MASKED)
    total[...] = jnp.zeros_like(total)
    mix[...] = jnp.zeros_like(mix)
    own_marks = q_marks[:, :1]

    def absorb(h, keys, values, seen):
        scores = lax.dot_general(
            query[h], keys, (((1,), (1,)), ((), ())), preferred_element_type=jnp.float32
        )
        scores = jnp.where(seen, scores, MASKED)
        before = top[h]
        now = jnp.maximum(before, jnp.max(scores, axis=1, keepdims=True))
        fade = jnp.exp2(before - now)
        shares = jnp.exp2(scores - now[:, :1])
        total[h] = total[h] * fade + jnp.sum(shares, axis=1, keepdims=True)
        mix[h] = mix[h] * fade + jnp.dot(
            shares.astype(jnp.bfloat16), values, preferred_element_type=jnp.float32
        )
        top[h] = now

    def over_prefix(i, _):
        def on(k, *actions):
            @pl.when(i == k)
            def _():
                for action in actions:
                    action()

        for k in range(16):
            if k in before_block:
                on(k, *before_block[k])
        group, beside = i // 4, (i // 2) % 2
        turn_y = jnp.where(group == 0, 0, jnp.where(group == 3, 2, 3 - 2 * beside))
        turn_x = jnp.where(group == 1, 0, jnp.where(group == 2, 1, beside))
        at = ctx_of((y + turn_y) % 4, (xh + turn_x) % 2, (core + i % 2) % 2)
        marks = row_of(cache[at, 2 * span :], 0, span // HD)
        seen = marks <= own_marks
        for h in range(heads):
            absorb(h, cache[at, :span], cache[at, span : 2 * span], seen)
        return 0

    def sib(ring, *numbers):
        def wait():
            for k in numbers:
                ring.sib[k].wait_recv()

        return wait

    def start_out():
        turn.finish()
        out_ring.send_own()
        out_ring.send_across()

    before_block = {
        0: [sib(old_ring, 0, 1)],
        2: [lambda: sums.cross(2, -2)],
        3: [lambda: sums.step(1, (2,)), lambda: old_ring.near("side")],
        4: [sib(old_ring, 2, 3), turn.finish, out_ring.send_across],
        5: [lambda: sums.cross(1, -1, 0)],
        6: [lambda: sums.step(2, (0, 1)), old_ring.far],
        7: [out_ring.send_own],
        8: [sib(old_ring, 4, 5)],
        9: [lambda: sums.step(2, (2,))],
        11: [out_ring.send_side],
        12: [sib(old_ring, 6, 7), lambda: sums.step(3, (0, 1))],
        13: [lambda: out_ring.near("own")],
        15: [lambda: sums.step(3, (2,))],
    }
    lax.fori_loop(0, 16, over_prefix, 0)
    for copy in sent:
        copy.wait_recv()
    keep.wait()
    out_ring.near("side")
    for j in range(3):
        back = 2 - j
        row = row_of(cache[(c + 16 - back) % 16, 2 * span :], span // HD, rows // HD)
        row = jnp.where(c >= back, row, -1.0)
        same = row == own_marks
        if back == 0:
            at = lax.broadcasted_iota(jnp.int32, (rows, rows), 0)
            key_at = lax.broadcasted_iota(jnp.int32, (rows, rows), 1)
            same = same & (key_at <= at)
        for h in range(heads):
            absorb(h, fresh[0, j], fresh[1, j], same)
    for h in range(heads):
        attended[:, h * HD : (h + 1) * HD] = (mix[h] / total[h]).astype(jnp.bfloat16)

    ring = TpRing(net, attended, gathered, 208)
    gathered[t] = attended[...]
    ring.cross()
    sums.last_other()
    out_ring.far()
    ring.step(1)
    out_ring.finish()
    low, high = sums.last()
    half = rows // 2
    total_out[:half] = low + blocks[t, :half].astype(jnp.float32)
    total_out[half:] = high + blocks[t, half:].astype(jnp.float32)

    def project_out(j, _):
        b = arrival(j)
        part = out_rows[b // 2, b % 2].reshape(q_cols, stream.shape[1])
        total_out[...] += jnp.dot(gathered[b], part, preferred_element_type=jnp.float32)
        return 0

    ring.arrive(0, 1)
    lax.fori_loop(0, 2, project_out, 0)
    ring.step(2)
    ring.arrive(1, 3)
    lax.fori_loop(2, 6, project_out, 0)
    ring.step(3)
    ring.arrive(3, 5)
    lax.fori_loop(6, 10, project_out, 0)
    ring.step(4)
    ring.arrive(5, 7)
    lax.fori_loop(10, 14, project_out, 0)
    ring.arrive(7, 9)
    lax.fori_loop(14, 16, project_out, 0)
    output[...] = total_out[...].astype(jnp.bfloat16)
    net.drain()
    assert len(net.copies) <= COPIES


def run_block(stream, pending, w_query, w_key, w_value, w_out, old_keys, old_values, labels,
              gain, cosine, sinus):
    rows, cols = stream.shape
    depth, q_cols = w_query.shape
    span = old_keys.shape[1]
    low, wide = jnp.bfloat16, jnp.float32
    half = rows // 2
    any_spec = pl.BlockSpec(memory_space=pl.ANY)
    vmem = pl.BlockSpec(memory_space=pltpu.VMEM)
    heads = q_cols // HD
    return pl.pallas_call(
        block_kernel,
        out_shape=jax.ShapeDtypeStruct((rows, cols), low),
        in_specs=[any_spec] * 9 + [vmem] * 3,
        out_specs=vmem,
        scratch_shapes=[
            pltpu.VMEM((16, rows, cols), low),
            pltpu.VMEM((16, depth, q_cols + HD), low),
            pltpu.VMEM((16, 2 * span + LABEL_ROWS, HD), low),
            pltpu.VMEM((8, 2, 8, w_out.shape[0] // 8, w_out.shape[1]), low),
            pltpu.VMEM((16, rows, q_cols), low),
            pltpu.VMEM((16, rows, cols), low),
            pltpu.VMEM((8, half, cols), low),
            pltpu.VMEM((2, 3, 4, half, cols), low),
            pltpu.VMEM((2, half // 2, cols), low),
            pltpu.VMEM((half, cols), low),
            pltpu.VMEM((rows, q_cols + HD), wide),
            pltpu.VMEM((rows, HD), wide),
            pltpu.VMEM((heads, rows, HD), low),
            pltpu.VMEM((rows, HD), low),
            pltpu.VMEM((2, 3, rows, HD), low),
            pltpu.VMEM((8, w_out.shape[0] // 8, w_out.shape[1]), low),
            pltpu.VMEM((rows, q_cols), low),
            pltpu.VMEM((rows, cols), wide),
            pltpu.VMEM((rows, HD), wide),
            pltpu.VMEM((heads, rows, HD), wide),
            pltpu.VMEM((heads, rows, HD), wide),
            pltpu.VMEM((heads, rows, HD), wide),
            pltpu.SemaphoreType.DMA((8,)),
            pltpu.SemaphoreType.DMA((16,)),
            pltpu.SemaphoreType.DMA((COPIES,)),
            pltpu.SemaphoreType.DMA((COPIES,)),
            pltpu.SemaphoreType.DMA((4,)),
        ],
        compiler_params=pltpu.CompilerParams(
            collective_id=0, has_side_effects=True, vmem_limit_bytes=58 << 20
        ),
        name="attention_block",
    )(stream, pending, w_query, w_key, w_value, w_out, old_keys, old_values, labels,
      gain, cosine, sinus)


def per_device(
    stream,
    pending,
    norm_gain,
    w_query,
    w_key,
    w_value,
    w_out,
    prefix_keys,
    prefix_values,
    prefix_segments,
    stretch_segments,
    stretch_offset,
):
    rows, cols = stream.shape
    token = lax.axis_index("ctx") * rows + jnp.arange(rows, dtype=jnp.int32)
    positions = stretch_offset[0].astype(jnp.float32) + token.astype(jnp.float32)
    angles = positions[:, None] * inverse_freqs(HD)
    cosine, sinus = jnp.cos(angles), jnp.sin(angles)
    labels = jnp.concatenate([prefix_segments, stretch_segments]).reshape(-1, HD)
    labels = jnp.pad(labels, ((0, LABEL_ROWS - labels.shape[0]), (0, 0))).astype(jnp.bfloat16)
    gain = norm_gain.astype(jnp.float32).reshape(16, 1, cols)
    return run_block(
        stream, pending, w_query, w_key, w_value, w_out, prefix_keys, prefix_values, labels,
        gain, cosine, sinus,
    )


def solution(mesh):
    in_specs = (
        P("ctx", "tp"),
        P("tp", "ctx", None),
        P(),
        P("ctx", "tp"),
        P("ctx", None),
        P("ctx", None),
        P("tp", "ctx"),
        P(None, "ctx", None),
        P(None, "ctx", None),
        P("ctx"),
        P("ctx"),
        P(),
    )
    return jax.shard_map(
        per_device, mesh=mesh, in_specs=in_specs, out_specs=P("ctx", "tp"), check_vma=False
    )
```

```python
import functools
import math

import jax
import jax.numpy as jnp
import numpy as np
from jax import lax
from jax.experimental import pallas as pl
from jax.experimental.pallas import tpu as pltpu
from jax.sharding import PartitionSpec as P

MESH = pl.DeviceIdType.MESH
HD = 128
ROPE_BASE = 500000.0
ROPE_FACTOR = 8.0
LOW_FREQ = 1.0
HIGH_FREQ = 4.0
INITIAL_SPAN = 8192.0
NORM_EPSILON = 1e-05
MASKED = -1e30
LABEL_ROWS = 16


def inverse_freqs(head_width):
    pair_index = np.arange(head_width // 2, dtype=np.float64)
    base_freq = ROPE_BASE ** (-2.0 * pair_index / head_width)
    wavelength = 2.0 * math.pi / base_freq
    smooth = (INITIAL_SPAN / wavelength - LOW_FREQ) / (HIGH_FREQ - LOW_FREQ)
    blended = (1.0 - smooth) * base_freq / ROPE_FACTOR + smooth * base_freq
    chosen = np.where(
        wavelength < INITIAL_SPAN / HIGH_FREQ,
        base_freq,
        np.where(wavelength > INITIAL_SPAN / LOW_FREQ, base_freq / ROPE_FACTOR, blended),
    )
    return chosen.astype(np.float32)


def coords():
    c = lax.axis_index("ctx")
    t = lax.axis_index("tp")
    return c // 4, (c // 2) % 2, c % 2, t // 2, t % 2


def ctx_of(y, xh, core):
    return (y * 2 + xh) * 2 + core


def tp_of(z, xl):
    return z * 2 + xl


def neighbours():
    y, xh, core, z, xl = coords()
    here = ctx_of(y, xh, core)
    mine = tp_of(z, xl)
    return {
        "z+": (here, tp_of((z + 1) % 8, xl)),
        "z-": (here, tp_of((z + 7) % 8, xl)),
        "xl": (here, tp_of(z, 1 - xl)),
        "y+": (ctx_of((y + 1) % 4, xh, core), mine),
        "y-": (ctx_of((y + 3) % 4, xh, core), mine),
        "xh": (ctx_of(y, 1 - xh, core), mine),
        "xd": (ctx_of(y, 1 - xh, core), tp_of(z, 1 - xl)),
        "sib": (ctx_of(y, xh, 1 - core), mine),
    }


def greet(devices):
    barrier = pltpu.get_barrier_semaphore()
    for device in devices:
        pl.semaphore_signal(barrier, inc=1, device_id=device, device_id_type=MESH)
    pl.semaphore_wait(barrier, len(devices))


class Copy:
    def __init__(self, net, k, sent, ref, device):
        self.root, self.shape = getattr(ref, "ref", ref), ref.shape
        self.net, self.k, self.sent, self.device = net, k, sent, device

    def handle(self):
        lead = (0,) * (len(self.root.shape) - len(self.shape))
        like = self.root.at[(*lead, *(pl.ds(0, n) for n in self.shape))]
        return pltpu.make_async_remote_copy(
            src_ref=like,
            dst_ref=like,
            send_sem=self.net.send_sem.at[self.sent],
            recv_sem=self.net.recv_sem.at[self.k],
            device_id=self.device,
            device_id_type=MESH,
        )

    def wait_recv(self):
        self.handle().wait_recv()

    def wait_send(self):
        self.handle().wait_send()


class Net:
    def __init__(self, links, send_sem, recv_sem):
        self.links, self.send_sem, self.recv_sem = links, send_sem, recv_sem
        self.count, self.under_way, self.spare, self.used = 0, [], [], 0

    def push(self, src, link, dst=None):
        k, self.count = self.count, self.count + 1
        if self.spare:
            sent = self.spare.pop(0)
        else:
            sent, self.used = self.used, self.used + 1
        device = self.links[link] if isinstance(link, str) else link
        pltpu.make_async_remote_copy(
            src_ref=src,
            dst_ref=src if dst is None else dst,
            send_sem=self.send_sem.at[sent],
            recv_sem=self.recv_sem.at[k],
            device_id=device,
            device_id_type=MESH,
        ).start()
        self.under_way.append(Copy(self, k, sent, src, device))
        return self.under_way[-1]

    def drain(self, before=None):
        done = [copy for copy in self.under_way if before is None or copy.k < before]
        self.under_way = [copy for copy in self.under_way if copy not in done]
        for copy in done:
            copy.wait_send()
        self.spare += [copy.sent for copy in done]


class TpRing:
    def __init__(self, net, own, buf, upper):
        self.net, self.own, self.buf = net, own, buf
        half = own.shape[0] - upper
        part = -(-upper // 32) * 16
        self.low, self.high = pl.ds(0, half), pl.ds(half, upper)
        self.parts = (pl.ds(half, part), pl.ds(half + part, upper - part))
        _, _, _, z, xl = coords()
        t = tp_of(z, xl)
        self.swap = net.push(own.at[self.low], "xl", buf.at[t, self.low])
        self.hop = {}
        for way in ("z+", "z-"):
            self.hop[way, "own"] = net.push(own.at[self.low], way, buf.at[t, self.low])
            self.hop[way, "high"] = net.push(own.at[self.high], way, buf.at[t, self.high])
        self.across = []

    def cross(self):
        _, _, _, z, xl = coords()
        self.swap.wait_recv()
        for way in ("z+", "z-"):
            self.hop[way, "other"] = self.net.push(self.buf.at[tp_of(z, 1 - xl), self.low], way)
        self.across.append(
            self.net.push(self.own.at[self.high], "xl", self.buf.at[tp_of(z, xl), self.high])
        )

    def step(self, step):
        _, _, _, z, xl = coords()
        push, buf, hop = self.net.push, self.buf, self.hop
        for kind in ("own", "high", "other"):
            for way, sign in (("z+", -1), ("z-", 1)):
                at = (z + sign * step + 8) % 8
                mine, theirs = tp_of(at, xl), tp_of(at, 1 - xl)
                part = 0 if way == "z+" else 1
                if kind == "high":
                    hop[way, kind].wait_recv()
                    if step < 4:
                        rows = self.high if step < 3 else self.parts[part]
                        hop[way, kind] = push(buf.at[mine, rows], way)
                    rows = self.high if step < 4 else self.parts[part]
                    self.across.append(push(buf.at[mine, rows], "xl"))
                    continue
                last = part == (0 if kind == "own" else 1)
                if step < 4 or last:
                    hop[way, kind].wait_recv()
                if step < 3 or (step == 3 and last):
                    hop[way, kind] = push(buf.at[mine if kind == "own" else theirs, self.low], way)

    def arrive(self, first, last):
        for copy in self.across[first:last]:
            copy.wait_recv()


class CtxRing:
    def __init__(self, net, own, slot, side_link):
        self.net, self.own, self.slot, self.side_link = net, own, slot, side_link
        y, xh, core, _, _ = coords()
        self.c, self.beside = ctx_of(y, xh, core), ctx_of(y, 1 - xh, core)
        self.sib, self.hop = [], {}

    def send_across(self):
        self.side = self.net.push(self.own, self.side_link, self.slot(self.c))
        self.sib.append(self.net.push(self.own, "sib", self.slot(self.c)))

    def send_own(self):
        for way in ("y+", "y-"):
            self.hop[way, "own"] = self.net.push(self.own, way, self.slot(self.c))

    def send_side(self):
        self.side.wait_recv()
        for way in ("y+", "y-"):
            self.hop[way, "side"] = self.net.push(self.slot(self.beside), way)
        self.sib.append(self.net.push(self.slot(self.beside), "sib"))

    def came(self, way, step, kind):
        y, xh, core, _, _ = coords()
        at = (y + (-step if way == "y+" else step) + 4) % 4
        self.hop[way, kind].wait_recv()
        return self.slot(ctx_of(at, xh if kind == "own" else 1 - xh, core))

    def near(self, kind):
        for way in ("y+", "y-"):
            block = self.came(way, 1, kind)
            if (way == "y+") == (kind == "own"):
                self.hop[way, kind] = self.net.push(block, way)
            self.sib.append(self.net.push(block, "sib"))

    def far(self):
        for way, kind in (("y+", "own"), ("y-", "side")):
            self.sib.append(self.net.push(self.came(way, 2, kind), "sib"))

    def finish(self):
        for copy in self.sib:
            copy.wait_recv()


class Turn:
    def __init__(self, net, w_out, mid, turned, sems):
        self.net, self.w_out, self.mid, self.turned, self.sems = net, w_out, mid, turned, sems
        y, xh, core, z, xl = coords()
        self.eighth = y * 2 + xh
        self.rows = w_out.shape[0] // 8
        self.stays = core == xl

    def place(self, ahead):
        _, _, core, z, xl = coords()
        at = (self.eighth + ahead) % 8
        return (at * 2 + xl, tp_of(z, core))

    def height(self, ahead):
        _, _, _, z, xl = coords()
        c = lax.axis_index("ctx")
        return (c, tp_of((z + ahead) % 8, xl))

    def first(self):
        src = self.w_out.at[pl.ds(pl.multiple_of(self.eighth * self.rows, self.rows), self.rows)]
        dst = self.mid.at[self.eighth]
        away = pltpu.make_async_remote_copy(
            src_ref=src,
            dst_ref=dst,
            send_sem=self.sems.at[0],
            recv_sem=self.sems.at[1],
            device_id=self.place(0),
            device_id_type=MESH,
        )
        return away, pltpu.make_async_copy(src, dst, self.sems.at[2])

    def spread(self):
        away, stay = self.first()
        pl.when(jnp.logical_not(self.stays))(away.start)
        pl.when(self.stays)(stay.start)
        self.got = []
        for ahead in range(1, 8):
            at = (self.eighth + ahead) % 8
            src = self.w_out.at[pl.ds(pl.multiple_of(at * self.rows, self.rows), self.rows)]
            self.got.append(self.net.push(src, self.place(ahead), self.mid.at[self.eighth]))

    def own(self, z):
        core = lax.axis_index("ctx") % 2
        return self.turned.at[z, core, self.eighth]

    def rise(self):
        away, stay = self.first()

        @pl.when(jnp.logical_not(self.stays))
        def _():
            away.wait_send()
            away.wait_recv()

        pl.when(self.stays)(stay.wait)
        for copy in self.got:
            copy.wait_recv()
        _, _, _, z, _ = coords()
        keep = pltpu.make_async_copy(self.mid.at[z], self.own(z), self.sems.at[3])
        keep.start()
        self.risen = [
            self.net.push(self.mid.at[(z + ahead) % 8], self.height(ahead), self.own(z))
            for ahead in range(1, 8)
        ]

    def finish(self):
        _, _, _, z, _ = coords()
        pltpu.make_async_copy(self.mid.at[z], self.own(z), self.sems.at[3]).wait()
        for copy in self.risen:
            copy.wait_recv()


class PendingSum:
    def __init__(
        self, net, pending, slabs, crossed, landed, landed_high, landed_parts, final, sems
    ):
        self.net, self.slabs, self.crossed = net, slabs, crossed
        self.landed, self.landed_high = landed, landed_high
        self.landed_parts, self.final = landed_parts, final
        _, _, _, self.z, self.xl = coords()
        rows, cols = slabs.shape[1:]
        upper, part = crossed.shape[1], landed_parts.shape[1]
        self.half = rows - upper
        self.low, self.high = pl.ds(0, self.half), pl.ds(self.half, upper)
        self.parts = (pl.ds(self.half, part), pl.ds(self.half + part, upper - part))
        self.loads = [
            pltpu.make_async_copy(
                pending.at[0, :, pl.ds(k * cols, cols)], slabs.at[k], sems.at[k]
            )
            for k in range(16)
        ]
        for load in self.loads:
            load.start()
        self.hop, self.over = {}, {}

    def at(self, offset, other=0):
        return tp_of((self.z + offset + 8) % 8, (self.xl + other) % 2)

    def ready(self):
        for load in self.loads:
            load.wait()

    def cross(self, *offsets):
        for offset in offsets:
            slot = (self.z + offset + 8) % 8
            self.over[offset] = self.net.push(
                self.slabs.at[self.at(offset, 1), self.high], "xl", self.crossed.at[slot]
            )

    def add(self, index, rows, more):
        total = self.slabs[index, rows].astype(jnp.float32) + more.astype(jnp.float32)
        self.slabs[index, rows] = total.astype(jnp.bfloat16)

    def take_crossed(self, offset):
        self.over[offset].wait_recv()
        slot = (self.z + offset + 8) % 8
        self.add(self.at(offset), self.high, self.crossed[slot])

    def land(self, way, kind, step):
        if kind == 2 and step == 0:
            return self.landed_parts.at[way]
        if kind == 2:
            return self.landed_high.at[way, step - 1]
        return self.landed.at[way, kind, step]

    def send(self, way, kind, step, index, rows):
        self.hop[way, kind] = self.net.push(
            self.slabs.at[index, rows], ("z+", "z-")[way], self.land(way, kind, step)
        )

    def first(self):
        self.send(0, 0, 0, self.at(4), self.low)
        self.send(1, 1, 0, self.at(4, 1), self.low)

    def first_high(self):
        self.take_crossed(4)
        for way in (0, 1):
            self.send(way, 2, 0, self.at(4), self.parts[way])

    def step(self, step, kinds):
        for way, sign in ((0, 1), (1, -1)):
            offset = sign * (4 - step)
            for kind in kinds:
                index = self.at(offset, 1 if kind == 1 else 0)
                rows = self.high if kind == 2 else self.low
                if kind == 2:
                    self.take_crossed(offset)
                if step > 1 or kind == 2 or kind == way:
                    self.hop[way, kind].wait_recv()
                    into = self.parts[way] if kind == 2 and step == 1 else rows
                    self.add(index, into, self.land(way, kind, step - 1)[...])
                self.send(way, kind, step, index, rows)

    def last_other(self):
        for way in (0, 1):
            self.hop[way, 1].wait_recv()
        more = self.landed[0, 1, 3].astype(jnp.float32) + self.landed[1, 1, 3].astype(jnp.float32)
        self.add(self.at(0, 1), self.low, more)
        self.fold = self.net.push(self.slabs.at[self.at(0, 1), self.low], "xl", self.final)

    def last(self):
        wide = jnp.float32
        for way in (0, 1):
            self.hop[way, 0].wait_recv()
            self.hop[way, 2].wait_recv()
        self.over[0].wait_recv()
        self.fold.wait_recv()
        low = self.slabs[self.at(0), self.low].astype(wide) + self.final[...].astype(wide)
        low = low + self.landed[0, 0, 3].astype(wide) + self.landed[1, 0, 3].astype(wide)
        high = self.slabs[self.at(0), self.high].astype(wide) + self.crossed[self.z].astype(wide)
        high = high + self.landed_high[0, 2].astype(wide) + self.landed_high[1, 2].astype(wide)
        return low, high


COPIES = 159
UPPER = 192
SENDS = 87


def block_kernel(
    stream, pending, w_query, w_key, w_value, w_out, old_keys, old_values,
    prefix_labels, stretch_labels, gain, freqs, offset,
    output,
    blocks, weights, cache, out_rows, gathered,
    slabs, crossed, landed, landed_high, landed_parts, final,
    totals, squares, query, made, fresh, mid, attended, total_out, q_marks, labels, cosine, sinus, gains,
    top, total, mix,
    local_sem, label_sem, load_sem, send_sem, recv_sem, turn_sem,
):
    y, xh, core, z, xl = coords()
    c, t = ctx_of(y, xh, core), tp_of(z, xl)
    rows = stream.shape[0]
    span = old_keys.shape[1]
    q_cols = w_query.shape[1]
    heads = q_cols // HD

    def row_of(marks, first, count):
        wide = marks.astype(jnp.float32)
        return jnp.concatenate([wide[first + k : first + k + 1] for k in range(count)], axis=1)

    def arrival(j):
        away = (j + 2) // 4
        sign = 1 - 2 * (((j + 2) // 2) % 2)
        return tp_of((z + sign * away + 8) % 8, (xl + j % 2) % 2)

    local = [
        pltpu.make_async_copy(stream, blocks.at[t], local_sem.at[0]),
        pltpu.make_async_copy(w_query, weights.at[c, :, pl.ds(0, q_cols)], local_sem.at[1]),
        pltpu.make_async_copy(old_keys.at[z], cache.at[c, pl.ds(0, span)], local_sem.at[2]),
        pltpu.make_async_copy(old_values.at[z], cache.at[c, pl.ds(span, span)], local_sem.at[3]),
    ]
    marks_here = [
        pltpu.make_async_copy(ref.at[pl.ds(k * HD, HD)], labels.at[row], label_sem.at[row])
        for ref, k, row in [(prefix_labels, k, k) for k in range(span // HD)]
        + [(stretch_labels, k, span // HD + k) for k in range(rows // HD)]
    ]
    head_cols = pl.ds(pl.multiple_of(z * HD, HD), HD)
    kv_slot = weights.at[c, :, pl.ds(q_cols, HD)]
    key_copy = pltpu.make_async_copy(w_key.at[:, head_cols], kv_slot, local_sem.at[5])
    value_copy = pltpu.make_async_copy(w_value.at[:, head_cols], kv_slot, local_sem.at[5])
    labels[...] = jnp.zeros_like(labels)
    for copy in local + marks_here:
        copy.start()

    @pl.when(xl == 0)
    def _():
        key_copy.start()

    @pl.when(xl == 1)
    def _():
        value_copy.start()

    links = neighbours()
    later = {}
    for ahead in (1, 2):
        for other in (0, 1):
            later[ahead, other] = ((c + ahead) % 16, tp_of(z, (xl + other) % 2))
    earlier = [
        ((c + 16 - ahead) % 16, tp_of(z, (xl + other) % 2)) for ahead in (1, 2) for other in (0, 1)
    ]
    net = Net(links, send_sem, recv_sem)
    turn = Turn(net, w_out, mid, out_rows, turn_sem)
    peers = list(links.values()) + list(later.values()) + earlier
    peers += [turn.place(ahead) for ahead in range(1, 8)]
    peers += [turn.height(ahead) for ahead in range(2, 7)]
    barrier = pltpu.get_barrier_semaphore()
    for device in peers:
        pl.semaphore_signal(barrier, inc=1, device_id=device, device_id_type=MESH)

    @pl.when(core != xl)
    def _():
        pl.semaphore_signal(barrier, inc=1, device_id=turn.place(0), device_id_type=MESH)
        pl.semaphore_wait(barrier, len(peers) + 1)

    @pl.when(core == xl)
    def _():
        pl.semaphore_wait(barrier, len(peers))

    tp_ring = TpRing(net, stream, blocks, 176)
    local[1].wait()
    key_copy.wait()
    w_ring = CtxRing(net, weights.at[c], lambda k: weights.at[k], "xh")
    w_ring.send_own()
    w_ring.send_across()
    for copy in local[2:] + marks_here:
        copy.wait()
    cache[c, 2 * span :] = labels[...].astype(jnp.float32).astype(jnp.bfloat16)
    old_ring = CtxRing(net, cache.at[c], lambda k: cache.at[k], "xd")
    out_ring = CtxRing(
        net, turn.own(pl.ds(0, 8)), lambda k: out_rows.at[:, k % 2, k // 2], "xh"
    )
    sums = PendingSum(net, pending, slabs, crossed, landed, landed_high, landed_parts, final, load_sem)
    row = row_of(cache[c, 2 * span :], span // HD, rows // HD)
    flat = (rows, rows)
    diagonal = lax.broadcasted_iota(jnp.int32, flat, 0) == lax.broadcasted_iota(jnp.int32, flat, 1)
    q_marks[...] = jnp.sum(jnp.where(diagonal, row, 0.0), axis=1, keepdims=True) + jnp.zeros(
        (rows, HD), jnp.float32
    )
    token = (c * rows + lax.broadcasted_iota(jnp.int32, (rows, HD), 0)).astype(jnp.float32)
    angles = (offset[0].astype(jnp.float32) + token) * freqs[...]
    turns = jnp.floor(angles * (0.5 / math.pi) + 0.5)
    angles = (angles - turns * 6.28125) - turns * (2.0 * math.pi - 6.28125)
    cosine[...] = jnp.cos(angles)
    lower = lax.broadcasted_iota(jnp.int32, (rows, HD), 1) < HD // 2
    sinus[...] = jnp.where(lower, -1.0, 1.0) * jnp.sin(angles)
    wide_gain = gain[...].astype(jnp.float32)
    per_block = stream.shape[1] // HD
    for b in range(16):
        gains[b] = row_of(wide_gain, b * per_block, per_block)
    totals[...] = jnp.zeros_like(totals)
    squares[...] = jnp.zeros_like(squares)
    tp_ring.cross()
    turn.spread()
    w_ring.near("own")
    tp_ring.step(1)
    w_ring.send_side()
    old_ring.send_across()
    tp_ring.step(2)
    w_ring.near("side")
    w_ring.far()
    early = net.count
    old_ring.send_own()
    old_ring.send_side()
    tp_ring.step(3)
    sums.ready()
    sums.cross(4)
    w_ring.finish()
    tp_ring.arrive(0, 5)
    local[0].wait()

    def project(j, _):
        b = arrival(j)
        wide = blocks[b].astype(jnp.float32)
        part = wide * wide
        squares[...] += sum(part[:, k * HD : (k + 1) * HD] for k in range(part.shape[1] // HD))
        low = (wide * gains[b]).astype(jnp.bfloat16)
        totals[...] += jnp.dot(low, weights[b], preferred_element_type=jnp.float32)
        return 0

    lax.fori_loop(0, 10, project, 0)
    tp_ring.step(4)
    sums.first()
    sums.first_high()
    turn.rise()
    old_ring.near("own")
    tp_ring.arrive(5, 9)
    sums.cross(3, -3)
    lax.fori_loop(10, 16, project, 0)
    width = 16 * stream.shape[1]
    mean_square = jnp.sum(squares[...], axis=1, keepdims=True) / width
    scale = lax.rsqrt(mean_square + NORM_EPSILON)
    def rotate(part):
        return part * cosine[...] + pltpu.roll(part, HD // 2, 1) * sinus[...]

    part = totals[:, 2 * HD :] * scale

    @pl.when(xl == 0)
    def _():
        made[...] = rotate(part).astype(jnp.bfloat16)

    @pl.when(xl == 1)
    def _():
        made[...] = part.astype(jnp.bfloat16)

    keep = pltpu.make_async_copy(made, fresh.at[xl, 2], local_sem.at[7])
    keep.start()
    sent = [net.push(made, "xl", fresh.at[xl, 2])]
    for (ahead, _), device in later.items():
        sent.append(net.push(made, device, fresh.at[xl, 2 - ahead]))
    sums.step(1, (0, 1))

    to_exponent = math.log2(math.e) / math.sqrt(HD)
    for h in range(heads):
        part = totals[:, h * HD : (h + 1) * HD] * scale
        query[h] = (rotate(part) * to_exponent).astype(jnp.bfloat16)

    net.drain(early)
    early = net.count
    top[...] = jnp.full_like(top, MASKED)
    total[...] = jnp.zeros_like(total)
    mix[...] = jnp.zeros_like(mix)
    own_marks = q_marks[:, :1]

    def absorb(h, keys, values, seen):
        scores = lax.dot_general(
            query[h], keys, (((1,), (1,)), ((), ())), preferred_element_type=jnp.float32
        )
        scores = jnp.where(seen, scores, MASKED)
        before = top[h]
        now = jnp.maximum(before, jnp.max(scores, axis=1, keepdims=True))
        fade = jnp.exp2(before - now)
        shares = jnp.exp2(scores - now[:, :1])
        total[h] = total[h] * fade + jnp.sum(shares, axis=1, keepdims=True)
        mix[h] = mix[h] * fade + jnp.dot(
            shares.astype(jnp.bfloat16), values, preferred_element_type=jnp.float32
        )
        top[h] = now

    def over_prefix(i, _):
        def on(k, *actions):
            @pl.when(i == k)
            def _():
                for action in actions:
                    action()

        for k in range(16):
            if k in before_block:
                on(k, *before_block[k])
        group, beside = i // 4, (i // 2) % 2
        turn_y = jnp.where(group == 0, 0, jnp.where(group == 3, 2, 3 - 2 * beside))
        turn_x = jnp.where(group == 1, 0, jnp.where(group == 2, 1, beside))
        at = ctx_of((y + turn_y) % 4, (xh + turn_x) % 2, (core + i % 2) % 2)
        marks = row_of(cache[at, 2 * span :], 0, span // HD)
        seen = marks <= own_marks
        for h in range(heads):
            absorb(h, cache[at, :span], cache[at, span : 2 * span], seen)
        return 0

    def sib(ring, *numbers):
        def wait():
            for k in numbers:
                ring.sib[k].wait_recv()

        return wait

    def start_out():
        turn.finish()
        out_ring.send_own()
        out_ring.send_across()

    before_block = {
        0: [sib(old_ring, 0, 1)],
        1: [lambda: sums.cross(2, -2)],
        4: [lambda: sums.step(1, (2,)), lambda: old_ring.near("side"), sib(old_ring, 2, 3)],
        5: [turn.finish, out_ring.send_across],
        6: [lambda: sums.step(2, (0, 1)), old_ring.far],
        7: [out_ring.send_own],
        8: [sib(old_ring, 4, 5)],
        9: [lambda: sums.step(2, (2,)), lambda: sums.cross(1, -1, 0)],
        11: [lambda: sums.step(3, (0, 1))],
        12: [sib(old_ring, 6, 7)],
        13: [out_ring.send_side],
        14: [lambda: out_ring.near("own")],
        15: [lambda: sums.step(3, (2,))],
    }
    lax.fori_loop(0, 16, over_prefix, 0)
    for copy in sent:
        copy.wait_recv()
    keep.wait()
    out_ring.near("side")
    for j in range(3):
        back = 2 - j
        row = row_of(cache[(c + 16 - back) % 16, 2 * span :], span // HD, rows // HD)
        row = jnp.where(c >= back, row, -1.0)
        same = row == own_marks
        if back == 0:
            at = lax.broadcasted_iota(jnp.int32, (rows, rows), 0)
            key_at = lax.broadcasted_iota(jnp.int32, (rows, rows), 1)
            same = same & (key_at <= at)
        for h in range(heads):
            absorb(h, fresh[0, j], fresh[1, j], same)
    for h in range(heads):
        attended[:, h * HD : (h + 1) * HD] = (mix[h] / total[h]).astype(jnp.bfloat16)

    net.drain(early)
    ring = TpRing(net, attended, gathered, 208)
    gathered[t] = attended[...]
    ring.cross()
    sums.last_other()
    out_ring.far()
    ring.step(1)
    out_ring.finish()
    low, high = sums.last()
    total_out[: sums.half] = low + blocks[t, : sums.half].astype(jnp.float32)
    total_out[sums.half :] = high + blocks[t, sums.half :].astype(jnp.float32)

    def project_out(j, _):
        b = arrival(j)
        part = out_rows[b // 2, b % 2].reshape(q_cols, stream.shape[1])
        total_out[...] += jnp.dot(gathered[b], part, preferred_element_type=jnp.float32)
        return 0

    ring.arrive(0, 1)
    lax.fori_loop(0, 2, project_out, 0)
    ring.step(2)
    ring.arrive(1, 3)
    lax.fori_loop(2, 6, project_out, 0)
    ring.step(3)
    ring.arrive(3, 5)
    lax.fori_loop(6, 10, project_out, 0)
    ring.step(4)
    ring.arrive(5, 7)
    lax.fori_loop(10, 14, project_out, 0)
    ring.arrive(7, 9)
    lax.fori_loop(14, 16, project_out, 0)
    output[...] = total_out[...].astype(jnp.bfloat16)
    net.drain()
    assert net.count == COPIES and net.used == SENDS, (net.count, net.used)


def run_block(stream, pending, w_query, w_key, w_value, w_out, old_keys, old_values,
              prefix_labels, stretch_labels, gain, freqs, offset):
    rows, cols = stream.shape
    depth, q_cols = w_query.shape
    span = old_keys.shape[1]
    low, wide = jnp.bfloat16, jnp.float32
    any_spec = pl.BlockSpec(memory_space=pl.ANY)
    vmem = pl.BlockSpec(memory_space=pltpu.VMEM)
    heads = q_cols // HD
    return pl.pallas_call(
        block_kernel,
        out_shape=jax.ShapeDtypeStruct((rows, cols), low),
        in_specs=[any_spec] * 10 + [vmem] * 2 + [pl.BlockSpec(memory_space=pltpu.SMEM)],
        out_specs=vmem,
        scratch_shapes=[
            pltpu.VMEM((16, rows, cols), low),
            pltpu.VMEM((16, depth, q_cols + HD), low),
            pltpu.VMEM((16, 2 * span + LABEL_ROWS, HD), low),
            pltpu.VMEM((8, 2, 8, w_out.shape[0] // 8, w_out.shape[1]), low),
            pltpu.VMEM((16, rows, q_cols), low),
            pltpu.VMEM((16, rows, cols), low),
            pltpu.VMEM((8, UPPER, cols), low),
            pltpu.VMEM((2, 2, 4, rows - UPPER, cols), low),
            pltpu.VMEM((2, 3, UPPER, cols), low),
            pltpu.VMEM((2, UPPER // 2, cols), low),
            pltpu.VMEM((rows - UPPER, cols), low),
            pltpu.VMEM((rows, q_cols + HD), wide),
            pltpu.VMEM((rows, HD), wide),
            pltpu.VMEM((heads, rows, HD), low),
            pltpu.VMEM((rows, HD), low),
            pltpu.VMEM((2, 3, rows, HD), low),
            pltpu.VMEM((8, w_out.shape[0] // 8, w_out.shape[1]), low),
            pltpu.VMEM((rows, q_cols), low),
            pltpu.VMEM((rows, cols), wide),
            pltpu.VMEM((rows, HD), wide),
            pltpu.VMEM((LABEL_ROWS, HD), jnp.int32),
            pltpu.VMEM((rows, HD), wide),
            pltpu.VMEM((rows, HD), wide),
            pltpu.VMEM((16, 1, cols), wide),
            pltpu.VMEM((heads, rows, HD), wide),
            pltpu.VMEM((heads, rows, HD), wide),
            pltpu.VMEM((heads, rows, HD), wide),
            pltpu.SemaphoreType.DMA((8,)),
            pltpu.SemaphoreType.DMA((LABEL_ROWS,)),
            pltpu.SemaphoreType.DMA((16,)),
            pltpu.SemaphoreType.DMA((SENDS,)),
            pltpu.SemaphoreType.DMA((COPIES,)),
            pltpu.SemaphoreType.DMA((4,)),
        ],
        compiler_params=pltpu.CompilerParams(
            collective_id=0, has_side_effects=True, vmem_limit_bytes=58 << 20
        ),
        name="attention_block",
    )(stream, pending, w_query, w_key, w_value, w_out, old_keys, old_values,
      prefix_labels, stretch_labels, gain, freqs, offset)


def per_device(
    stream,
    pending,
    norm_gain,
    w_query,
    w_key,
    w_value,
    w_out,
    prefix_keys,
    prefix_values,
    prefix_segments,
    stretch_segments,
    stretch_offset,
):
    freqs = inverse_freqs(HD)
    return run_block(
        stream, pending, w_query, w_key, w_value, w_out, prefix_keys, prefix_values,
        prefix_segments, stretch_segments, norm_gain.reshape(-1, HD),
        jnp.asarray(np.concatenate([freqs, freqs])[None]), stretch_offset,
    )


def solution(mesh):
    in_specs = (
        P("ctx", "tp"),
        P("tp", "ctx", None),
        P(),
        P("ctx", "tp"),
        P("ctx", None),
        P("ctx", None),
        P("tp", "ctx"),
        P(None, "ctx", None),
        P(None, "ctx", None),
        P("ctx"),
        P("ctx"),
        P(),
    )
    return jax.shard_map(
        per_device, mesh=mesh, in_specs=in_specs, out_specs=P("ctx", "tp"), check_vma=False
    )
```

```python
import functools
import math

import jax
import jax.numpy as jnp
import numpy as np
from jax import lax
from jax.experimental import pallas as pl
from jax.experimental.pallas import tpu as pltpu
from jax.sharding import PartitionSpec as P

MESH = pl.DeviceIdType.MESH
HD = 128
ROPE_BASE = 500000.0
ROPE_FACTOR = 8.0
LOW_FREQ = 1.0
HIGH_FREQ = 4.0
INITIAL_SPAN = 8192.0
NORM_EPSILON = 1e-05
MASKED = -1e30
LABEL_ROWS = 16


def inverse_freqs(head_width):
    pair_index = np.arange(head_width // 2, dtype=np.float64)
    base_freq = ROPE_BASE ** (-2.0 * pair_index / head_width)
    wavelength = 2.0 * math.pi / base_freq
    smooth = (INITIAL_SPAN / wavelength - LOW_FREQ) / (HIGH_FREQ - LOW_FREQ)
    blended = (1.0 - smooth) * base_freq / ROPE_FACTOR + smooth * base_freq
    chosen = np.where(
        wavelength < INITIAL_SPAN / HIGH_FREQ,
        base_freq,
        np.where(wavelength > INITIAL_SPAN / LOW_FREQ, base_freq / ROPE_FACTOR, blended),
    )
    return chosen.astype(np.float32)


def coords():
    c = lax.axis_index("ctx")
    t = lax.axis_index("tp")
    return c // 4, (c // 2) % 2, c % 2, t // 2, t % 2


def ctx_of(y, xh, core):
    return (y * 2 + xh) * 2 + core


def tp_of(z, xl):
    return z * 2 + xl


def neighbours():
    y, xh, core, z, xl = coords()
    here = ctx_of(y, xh, core)
    mine = tp_of(z, xl)
    return {
        "z+": (here, tp_of((z + 1) % 8, xl)),
        "z-": (here, tp_of((z + 7) % 8, xl)),
        "xl": (here, tp_of(z, 1 - xl)),
        "y+": (ctx_of((y + 1) % 4, xh, core), mine),
        "y-": (ctx_of((y + 3) % 4, xh, core), mine),
        "xh": (ctx_of(y, 1 - xh, core), mine),
        "xd": (ctx_of(y, 1 - xh, core), tp_of(z, 1 - xl)),
        "sib": (ctx_of(y, xh, 1 - core), mine),
    }


def greet(devices):
    barrier = pltpu.get_barrier_semaphore()
    for device in devices:
        pl.semaphore_signal(barrier, inc=1, device_id=device, device_id_type=MESH)
    pl.semaphore_wait(barrier, len(devices))


class Copy:
    def __init__(self, net, k, sent, ref, device):
        self.root, self.shape = getattr(ref, "ref", ref), ref.shape
        self.net, self.k, self.sent, self.device = net, k, sent, device

    def handle(self):
        lead = (0,) * (len(self.root.shape) - len(self.shape))
        like = self.root.at[(*lead, *(pl.ds(0, n) for n in self.shape))]
        return pltpu.make_async_remote_copy(
            src_ref=like,
            dst_ref=like,
            send_sem=self.net.send_sem.at[self.sent],
            recv_sem=self.net.recv_sem.at[self.k],
            device_id=self.device,
            device_id_type=MESH,
        )

    def wait_recv(self):
        self.handle().wait_recv()

    def wait_send(self):
        self.handle().wait_send()


class Net:
    def __init__(self, links, send_sem, recv_sem):
        self.links, self.send_sem, self.recv_sem = links, send_sem, recv_sem
        self.count, self.under_way, self.spare, self.used = 0, [], [], 0

    def push(self, src, link, dst=None):
        k, self.count = self.count, self.count + 1
        if self.spare:
            sent = self.spare.pop(0)
        else:
            sent, self.used = self.used, self.used + 1
        device = self.links[link] if isinstance(link, str) else link
        pltpu.make_async_remote_copy(
            src_ref=src,
            dst_ref=src if dst is None else dst,
            send_sem=self.send_sem.at[sent],
            recv_sem=self.recv_sem.at[k],
            device_id=device,
            device_id_type=MESH,
        ).start()
        self.under_way.append(Copy(self, k, sent, src, device))
        return self.under_way[-1]

    def drain(self, before=None):
        done = [copy for copy in self.under_way if before is None or copy.k < before]
        self.under_way = [copy for copy in self.under_way if copy not in done]
        for copy in done:
            copy.wait_send()
        self.spare += [copy.sent for copy in done]


class TpRing:
    def __init__(self, net, own, buf, upper):
        self.net, self.own, self.buf = net, own, buf
        half = own.shape[0] - upper
        part = -(-upper // 32) * 16
        self.low, self.high = pl.ds(0, half), pl.ds(half, upper)
        self.parts = (pl.ds(half, part), pl.ds(half + part, upper - part))
        _, _, _, z, xl = coords()
        t = tp_of(z, xl)
        self.swap = net.push(own.at[self.low], "xl", buf.at[t, self.low])
        self.hop = {}
        for way in ("z+", "z-"):
            self.hop[way, "own"] = net.push(own.at[self.low], way, buf.at[t, self.low])
            self.hop[way, "high"] = net.push(own.at[self.high], way, buf.at[t, self.high])
        self.across = []

    def cross(self):
        _, _, _, z, xl = coords()
        self.swap.wait_recv()
        for way in ("z+", "z-"):
            self.hop[way, "other"] = self.net.push(self.buf.at[tp_of(z, 1 - xl), self.low], way)
        self.across.append(
            self.net.push(self.own.at[self.high], "xl", self.buf.at[tp_of(z, xl), self.high])
        )

    def step(self, step):
        _, _, _, z, xl = coords()
        push, buf, hop = self.net.push, self.buf, self.hop
        for kind in ("own", "high", "other"):
            for way, sign in (("z+", -1), ("z-", 1)):
                at = (z + sign * step + 8) % 8
                mine, theirs = tp_of(at, xl), tp_of(at, 1 - xl)
                part = 0 if way == "z+" else 1
                if kind == "high":
                    hop[way, kind].wait_recv()
                    if step < 4:
                        rows = self.high if step < 3 else self.parts[part]
                        hop[way, kind] = push(buf.at[mine, rows], way)
                    rows = self.high if step < 4 else self.parts[part]
                    self.across.append(push(buf.at[mine, rows], "xl"))
                    continue
                last = part == (0 if kind == "own" else 1)
                if step < 4 or last:
                    hop[way, kind].wait_recv()
                if step < 3 or (step == 3 and last):
                    hop[way, kind] = push(buf.at[mine if kind == "own" else theirs, self.low], way)

    def arrive(self, first, last):
        for copy in self.across[first:last]:
            copy.wait_recv()


class CtxRing:
    def __init__(self, net, own, slot, side_link):
        self.net, self.own, self.slot, self.side_link = net, own, slot, side_link
        y, xh, core, _, _ = coords()
        self.c, self.beside = ctx_of(y, xh, core), ctx_of(y, 1 - xh, core)
        self.sib, self.hop = [], {}

    def send_across(self):
        self.side = self.net.push(self.own, self.side_link, self.slot(self.c))
        self.sib.append(self.net.push(self.own, "sib", self.slot(self.c)))

    def send_own(self):
        for way in ("y+", "y-"):
            self.hop[way, "own"] = self.net.push(self.own, way, self.slot(self.c))

    def send_side(self):
        self.side.wait_recv()
        for way in ("y+", "y-"):
            self.hop[way, "side"] = self.net.push(self.slot(self.beside), way)
        self.sib.append(self.net.push(self.slot(self.beside), "sib"))

    def came(self, way, step, kind):
        y, xh, core, _, _ = coords()
        at = (y + (-step if way == "y+" else step) + 4) % 4
        self.hop[way, kind].wait_recv()
        return self.slot(ctx_of(at, xh if kind == "own" else 1 - xh, core))

    def near(self, kind):
        for way in ("y+", "y-"):
            block = self.came(way, 1, kind)
            if (way == "y+") == (kind == "own"):
                self.hop[way, kind] = self.net.push(block, way)
            self.sib.append(self.net.push(block, "sib"))

    def far(self):
        for way, kind in (("y+", "own"), ("y-", "side")):
            self.sib.append(self.net.push(self.came(way, 2, kind), "sib"))

    def finish(self):
        for copy in self.sib:
            copy.wait_recv()


class Turn:
    def __init__(self, net, w_out, mid, turned, sems):
        self.net, self.w_out, self.mid, self.turned, self.sems = net, w_out, mid, turned, sems
        y, xh, core, z, xl = coords()
        self.eighth = y * 2 + xh
        self.rows = w_out.shape[0] // 8
        self.stays = core == xl

    def place(self, ahead):
        _, _, core, z, xl = coords()
        at = (self.eighth + ahead) % 8
        return (at * 2 + xl, tp_of(z, core))

    def height(self, ahead):
        _, _, _, z, xl = coords()
        c = lax.axis_index("ctx")
        return (c, tp_of((z + ahead) % 8, xl))

    def first(self):
        src = self.w_out.at[pl.ds(pl.multiple_of(self.eighth * self.rows, self.rows), self.rows)]
        dst = self.mid.at[self.eighth]
        away = pltpu.make_async_remote_copy(
            src_ref=src,
            dst_ref=dst,
            send_sem=self.sems.at[0],
            recv_sem=self.sems.at[1],
            device_id=self.place(0),
            device_id_type=MESH,
        )
        return away, pltpu.make_async_copy(src, dst, self.sems.at[2])

    def spread(self):
        away, stay = self.first()
        pl.when(jnp.logical_not(self.stays))(away.start)
        pl.when(self.stays)(stay.start)
        self.got = []
        for ahead in range(1, 8):
            at = (self.eighth + ahead) % 8
            src = self.w_out.at[pl.ds(pl.multiple_of(at * self.rows, self.rows), self.rows)]
            self.got.append(self.net.push(src, self.place(ahead), self.mid.at[self.eighth]))

    def own(self, z):
        core = lax.axis_index("ctx") % 2
        return self.turned.at[z, core, self.eighth]

    def rise(self):
        away, stay = self.first()

        @pl.when(jnp.logical_not(self.stays))
        def _():
            away.wait_send()
            away.wait_recv()

        pl.when(self.stays)(stay.wait)
        for copy in self.got:
            copy.wait_recv()
        _, _, _, z, _ = coords()
        keep = pltpu.make_async_copy(self.mid.at[z], self.own(z), self.sems.at[3])
        keep.start()
        self.risen = [
            self.net.push(self.mid.at[(z + ahead) % 8], self.height(ahead), self.own(z))
            for ahead in range(1, 8)
        ]

    def finish(self):
        _, _, _, z, _ = coords()
        pltpu.make_async_copy(self.mid.at[z], self.own(z), self.sems.at[3]).wait()
        for copy in self.risen:
            copy.wait_recv()


class PendingSum:
    def __init__(
        self, net, pending, slabs, crossed, landed, landed_high, landed_parts, final, sems
    ):
        self.net, self.slabs, self.crossed = net, slabs, crossed
        self.landed, self.landed_high = landed, landed_high
        self.landed_parts, self.final = landed_parts, final
        _, _, _, self.z, self.xl = coords()
        rows, cols = slabs.shape[1:]
        upper, part = crossed.shape[1], landed_parts.shape[1]
        self.half = rows - upper
        self.low, self.high = pl.ds(0, self.half), pl.ds(self.half, upper)
        self.parts = (pl.ds(self.half, part), pl.ds(self.half + part, upper - part))
        self.loads = [
            pltpu.make_async_copy(
                pending.at[0, :, pl.ds(k * cols, cols)], slabs.at[k], sems.at[0]
            )
            for k in range(16)
        ]
        for load in self.loads:
            load.start()
        self.hop, self.over, self.sems = {}, {}, sems

    def at(self, offset, other=0):
        return tp_of((self.z + offset + 8) % 8, (self.xl + other) % 2)

    def ready(self):
        pltpu.make_async_copy(self.slabs, self.slabs, self.sems.at[0]).wait()

    def cross(self, *offsets):
        for offset in offsets:
            slot = (self.z + offset + 8) % 8
            self.over[offset] = self.net.push(
                self.slabs.at[self.at(offset, 1), self.high], "xl", self.crossed.at[slot]
            )

    def add(self, index, rows, more):
        total = self.slabs[index, rows].astype(jnp.float32) + more.astype(jnp.float32)
        self.slabs[index, rows] = total.astype(jnp.bfloat16)

    def take_crossed(self, offset):
        self.over[offset].wait_recv()
        slot = (self.z + offset + 8) % 8
        self.add(self.at(offset), self.high, self.crossed[slot])

    def land(self, way, kind, step):
        if kind == 2 and step == 0:
            return self.landed_parts.at[way]
        if kind == 2:
            return self.landed_high.at[way, step - 1]
        return self.landed.at[way, kind, step]

    def send(self, way, kind, step, index, rows):
        self.hop[way, kind] = self.net.push(
            self.slabs.at[index, rows], ("z+", "z-")[way], self.land(way, kind, step)
        )

    def first(self):
        self.send(0, 0, 0, self.at(4), self.low)
        self.send(1, 1, 0, self.at(4, 1), self.low)

    def first_high(self):
        self.take_crossed(4)
        for way in (0, 1):
            self.send(way, 2, 0, self.at(4), self.parts[way])

    def step(self, step, kinds):
        for way, sign in ((0, 1), (1, -1)):
            offset = sign * (4 - step)
            for kind in kinds:
                index = self.at(offset, 1 if kind == 1 else 0)
                rows = self.high if kind == 2 else self.low
                if kind == 2:
                    self.take_crossed(offset)
                if step > 1 or kind == 2 or kind == way:
                    self.hop[way, kind].wait_recv()
                    into = self.parts[way] if kind == 2 and step == 1 else rows
                    self.add(index, into, self.land(way, kind, step - 1)[...])
                self.send(way, kind, step, index, rows)

    def last_other(self):
        for way in (0, 1):
            self.hop[way, 1].wait_recv()
        more = self.landed[0, 1, 3].astype(jnp.float32) + self.landed[1, 1, 3].astype(jnp.float32)
        self.add(self.at(0, 1), self.low, more)
        self.fold = self.net.push(self.slabs.at[self.at(0, 1), self.low], "xl", self.final)

    def last(self):
        wide = jnp.float32
        for way in (0, 1):
            self.hop[way, 0].wait_recv()
            self.hop[way, 2].wait_recv()
        self.over[0].wait_recv()
        self.fold.wait_recv()
        low = self.slabs[self.at(0), self.low].astype(wide) + self.final[...].astype(wide)
        low = low + self.landed[0, 0, 3].astype(wide) + self.landed[1, 0, 3].astype(wide)
        high = self.slabs[self.at(0), self.high].astype(wide) + self.crossed[self.z].astype(wide)
        high = high + self.landed_high[0, 2].astype(wide) + self.landed_high[1, 2].astype(wide)
        return low, high


COPIES = 159
UPPER = 192
SENDS = 56


def block_kernel(
    stream, pending, w_query, w_key, w_value, w_out, old_keys, old_values,
    prefix_labels, stretch_labels, gain, freqs, offset,
    output,
    blocks, weights, cache, out_rows, gathered,
    slabs, crossed, landed, landed_high, landed_parts, final,
    totals, squares, query, made, fresh, mid, attended, total_out, q_marks, labels, cosine, sinus, gains,
    top, total, mix,
    local_sem, label_sem, load_sem, send_sem, recv_sem, turn_sem,
):
    y, xh, core, z, xl = coords()
    c, t = ctx_of(y, xh, core), tp_of(z, xl)
    rows = stream.shape[0]
    span = old_keys.shape[1]
    q_cols = w_query.shape[1]
    heads = q_cols // HD

    def row_of(marks, first, count):
        wide = marks.astype(jnp.float32)
        return jnp.concatenate([wide[first + k : first + k + 1] for k in range(count)], axis=1)

    def arrival(j):
        away = (j + 2) // 4
        sign = 1 - 2 * (((j + 2) // 2) % 2)
        return tp_of((z + sign * away + 8) % 8, (xl + j % 2) % 2)

    local = [
        pltpu.make_async_copy(stream, blocks.at[t], local_sem.at[0]),
        pltpu.make_async_copy(w_query, weights.at[c, :, pl.ds(0, q_cols)], local_sem.at[1]),
        pltpu.make_async_copy(old_keys.at[z], cache.at[c, pl.ds(0, span)], local_sem.at[2]),
        pltpu.make_async_copy(old_values.at[z], cache.at[c, pl.ds(span, span)], local_sem.at[3]),
    ]
    marks_here = [
        pltpu.make_async_copy(ref.at[pl.ds(k * HD, HD)], labels.at[row], label_sem.at[row])
        for ref, k, row in [(prefix_labels, k, k) for k in range(span // HD)]
        + [(stretch_labels, k, span // HD + k) for k in range(rows // HD)]
    ]
    head_cols = pl.ds(pl.multiple_of(z * HD, HD), HD)
    kv_slot = weights.at[c, :, pl.ds(q_cols, HD)]
    key_copy = pltpu.make_async_copy(w_key.at[:, head_cols], kv_slot, local_sem.at[5])
    value_copy = pltpu.make_async_copy(w_value.at[:, head_cols], kv_slot, local_sem.at[5])
    labels[...] = jnp.zeros_like(labels)
    for copy in local + marks_here:
        copy.start()

    @pl.when(xl == 0)
    def _():
        key_copy.start()

    @pl.when(xl == 1)
    def _():
        value_copy.start()

    links = neighbours()
    later = {}
    for ahead in (1, 2):
        for other in (0, 1):
            later[ahead, other] = ((c + ahead) % 16, tp_of(z, (xl + other) % 2))
    earlier = [
        ((c + 16 - ahead) % 16, tp_of(z, (xl + other) % 2)) for ahead in (1, 2) for other in (0, 1)
    ]
    net = Net(links, send_sem, recv_sem)
    turn = Turn(net, w_out, mid, out_rows, turn_sem)
    peers = list(links.values()) + list(later.values()) + earlier
    peers += [turn.place(ahead) for ahead in range(1, 8)]
    peers += [turn.height(ahead) for ahead in range(2, 7)]
    barrier = pltpu.get_barrier_semaphore()
    for device in peers:
        pl.semaphore_signal(barrier, inc=1, device_id=device, device_id_type=MESH)

    @pl.when(core != xl)
    def _():
        pl.semaphore_signal(barrier, inc=1, device_id=turn.place(0), device_id_type=MESH)
        pl.semaphore_wait(barrier, len(peers) + 1)

    @pl.when(core == xl)
    def _():
        pl.semaphore_wait(barrier, len(peers))

    tp_ring = TpRing(net, stream, blocks, 176)
    local[1].wait()
    key_copy.wait()
    w_ring = CtxRing(net, weights.at[c], lambda k: weights.at[k], "xh")
    w_ring.send_own()
    w_ring.send_across()
    for copy in local[2:] + marks_here:
        copy.wait()
    cache[c, 2 * span :] = labels[...].astype(jnp.float32).astype(jnp.bfloat16)
    old_ring = CtxRing(net, cache.at[c], lambda k: cache.at[k], "xd")
    out_ring = CtxRing(
        net, turn.own(pl.ds(0, 8)), lambda k: out_rows.at[:, k % 2, k // 2], "xh"
    )
    sums = PendingSum(net, pending, slabs, crossed, landed, landed_high, landed_parts, final, load_sem)
    row = row_of(cache[c, 2 * span :], span // HD, rows // HD)
    flat = (rows, rows)
    diagonal = lax.broadcasted_iota(jnp.int32, flat, 0) == lax.broadcasted_iota(jnp.int32, flat, 1)
    q_marks[...] = jnp.sum(jnp.where(diagonal, row, 0.0), axis=1, keepdims=True) + jnp.zeros(
        (rows, HD), jnp.float32
    )
    token = (c * rows + lax.broadcasted_iota(jnp.int32, (rows, HD), 0)).astype(jnp.float32)
    angles = (offset[0].astype(jnp.float32) + token) * freqs[...]
    turns = jnp.floor(angles * (0.5 / math.pi) + 0.5)
    angles = (angles - turns * 6.28125) - turns * (2.0 * math.pi - 6.28125)
    cosine[...] = jnp.cos(angles)
    lower = lax.broadcasted_iota(jnp.int32, (rows, HD), 1) < HD // 2
    sinus[...] = jnp.where(lower, -1.0, 1.0) * jnp.sin(angles)
    wide_gain = gain[...].astype(jnp.float32)
    per_block = stream.shape[1] // HD
    for b in range(16):
        gains[b] = row_of(wide_gain, b * per_block, per_block)
    totals[...] = jnp.zeros_like(totals)
    squares[...] = jnp.zeros_like(squares)
    tp_ring.cross()
    starts = net.count
    turn.spread()
    w_ring.near("own")
    tp_ring.step(1)
    w_ring.send_side()
    old_ring.send_across()
    first = net.count
    tp_ring.step(2)
    net.drain(starts)
    w_ring.near("side")
    w_ring.far()
    net.drain(first)
    early = net.count
    old_ring.send_own()
    old_ring.send_side()
    tp_ring.step(3)
    sums.ready()
    sums.cross(4)
    w_ring.finish()
    tp_ring.arrive(0, 5)
    local[0].wait()

    def project(j, _):
        b = arrival(j)
        wide = blocks[b].astype(jnp.float32)
        part = wide * wide
        squares[...] += sum(part[:, k * HD : (k + 1) * HD] for k in range(part.shape[1] // HD))
        low = (wide * gains[b]).astype(jnp.bfloat16)
        totals[...] += jnp.dot(low, weights[b], preferred_element_type=jnp.float32)
        return 0

    lax.fori_loop(0, 10, project, 0)
    tp_ring.step(4)
    net.drain(early)
    sums.first()
    sums.first_high()
    turn.rise()
    old_ring.near("own")
    tp_ring.arrive(5, 9)
    sums.cross(3, -3)
    lax.fori_loop(10, 16, project, 0)
    width = 16 * stream.shape[1]
    mean_square = jnp.sum(squares[...], axis=1, keepdims=True) / width
    scale = lax.rsqrt(mean_square + NORM_EPSILON)
    def rotate(part):
        return part * cosine[...] + pltpu.roll(part, HD // 2, 1) * sinus[...]

    part = totals[:, 2 * HD :] * scale

    @pl.when(xl == 0)
    def _():
        made[...] = rotate(part).astype(jnp.bfloat16)

    @pl.when(xl == 1)
    def _():
        made[...] = part.astype(jnp.bfloat16)

    keep = pltpu.make_async_copy(made, fresh.at[xl, 2], local_sem.at[7])
    keep.start()
    sent = [net.push(made, "xl", fresh.at[xl, 2])]
    for (ahead, _), device in later.items():
        sent.append(net.push(made, device, fresh.at[xl, 2 - ahead]))
    sums.step(1, (0, 1))

    to_exponent = math.log2(math.e) / math.sqrt(HD)
    for h in range(heads):
        part = totals[:, h * HD : (h + 1) * HD] * scale
        query[h] = (rotate(part) * to_exponent).astype(jnp.bfloat16)

    net.drain(early)
    sent_before = net.count
    top[...] = jnp.full_like(top, MASKED)
    total[...] = jnp.zeros_like(total)
    mix[...] = jnp.zeros_like(mix)
    own_marks = q_marks[:, :1]

    def absorb(h, keys, values, seen):
        scores = lax.dot_general(
            query[h], keys, (((1,), (1,)), ((), ())), preferred_element_type=jnp.float32
        )
        scores = jnp.where(seen, scores, MASKED)
        before = top[h]
        now = jnp.maximum(before, jnp.max(scores, axis=1, keepdims=True))
        fade = jnp.exp2(before - now)
        shares = jnp.exp2(scores - now[:, :1])
        total[h] = total[h] * fade + jnp.sum(shares, axis=1, keepdims=True)
        mix[h] = mix[h] * fade + jnp.dot(
            shares.astype(jnp.bfloat16), values, preferred_element_type=jnp.float32
        )
        top[h] = now

    def over_prefix(i, _):
        def on(k, *actions):
            @pl.when(i == k)
            def _():
                for action in actions:
                    action()

        for k in range(16):
            if k in before_block:
                on(k, *before_block[k])
        group, beside = i // 4, (i // 2) % 2
        turn_y = jnp.where(group == 0, 0, jnp.where(group == 3, 2, 3 - 2 * beside))
        turn_x = jnp.where(group == 1, 0, jnp.where(group == 2, 1, beside))
        at = ctx_of((y + turn_y) % 4, (xh + turn_x) % 2, (core + i % 2) % 2)
        marks = row_of(cache[at, 2 * span :], 0, span // HD)
        seen = marks <= own_marks
        for h in range(heads):
            absorb(h, cache[at, :span], cache[at, span : 2 * span], seen)
        return 0

    def sib(ring, *numbers):
        def wait():
            for k in numbers:
                ring.sib[k].wait_recv()

        return wait

    def start_out():
        turn.finish()
        out_ring.send_own()
        out_ring.send_across()

    before_block = {
        0: [sib(old_ring, 0, 1)],
        1: [lambda: sums.cross(2, -2)],
        4: [lambda: sums.step(1, (2,)), lambda: old_ring.near("side"), sib(old_ring, 2, 3)],
        5: [turn.finish, out_ring.send_across],
        6: [lambda: sums.step(2, (0, 1)), old_ring.far],
        7: [out_ring.send_own],
        8: [sib(old_ring, 4, 5)],
        9: [lambda: net.drain(sent_before), lambda: sums.step(2, (2,)), lambda: sums.cross(1, -1, 0)],
        11: [lambda: sums.step(3, (0, 1))],
        12: [sib(old_ring, 6, 7)],
        13: [out_ring.send_side],
        14: [lambda: out_ring.near("own")],
        15: [lambda: sums.step(3, (2,))],
    }
    lax.fori_loop(0, 16, over_prefix, 0)
    for copy in sent:
        copy.wait_recv()
    keep.wait()
    out_ring.near("side")
    for j in range(3):
        back = 2 - j
        row = row_of(cache[(c + 16 - back) % 16, 2 * span :], span // HD, rows // HD)
        row = jnp.where(c >= back, row, -1.0)
        same = row == own_marks
        if back == 0:
            at = lax.broadcasted_iota(jnp.int32, (rows, rows), 0)
            key_at = lax.broadcasted_iota(jnp.int32, (rows, rows), 1)
            same = same & (key_at <= at)
        for h in range(heads):
            absorb(h, fresh[0, j], fresh[1, j], same)
    for h in range(heads):
        attended[:, h * HD : (h + 1) * HD] = (mix[h] / total[h]).astype(jnp.bfloat16)

    net.drain(net.count - 16)
    ring = TpRing(net, attended, gathered, 208)
    gathered[t] = attended[...]
    ring.cross()
    sums.last_other()
    out_ring.far()
    ring.step(1)
    out_ring.finish()
    low, high = sums.last()
    total_out[: sums.half] = low + blocks[t, : sums.half].astype(jnp.float32)
    total_out[sums.half :] = high + blocks[t, sums.half :].astype(jnp.float32)

    def project_out(j, _):
        b = arrival(j)
        part = out_rows[b // 2, b % 2].reshape(q_cols, stream.shape[1])
        total_out[...] += jnp.dot(gathered[b], part, preferred_element_type=jnp.float32)
        return 0

    ring.arrive(0, 1)
    lax.fori_loop(0, 2, project_out, 0)
    ring.step(2)
    ring.arrive(1, 3)
    lax.fori_loop(2, 6, project_out, 0)
    ring.step(3)
    ring.arrive(3, 5)
    lax.fori_loop(6, 10, project_out, 0)
    ring.step(4)
    ring.arrive(5, 7)
    lax.fori_loop(10, 14, project_out, 0)
    ring.arrive(7, 9)
    lax.fori_loop(14, 16, project_out, 0)
    output[...] = total_out[...].astype(jnp.bfloat16)
    net.drain()
    assert net.count == COPIES and net.used == SENDS, (net.count, net.used)


def run_block(stream, pending, w_query, w_key, w_value, w_out, old_keys, old_values,
              prefix_labels, stretch_labels, gain, freqs, offset):
    rows, cols = stream.shape
    depth, q_cols = w_query.shape
    span = old_keys.shape[1]
    low, wide = jnp.bfloat16, jnp.float32
    any_spec = pl.BlockSpec(memory_space=pl.ANY)
    vmem = pl.BlockSpec(memory_space=pltpu.VMEM)
    heads = q_cols // HD
    return pl.pallas_call(
        block_kernel,
        out_shape=jax.ShapeDtypeStruct((rows, cols), low),
        in_specs=[any_spec] * 10 + [vmem] * 2 + [pl.BlockSpec(memory_space=pltpu.SMEM)],
        out_specs=vmem,
        scratch_shapes=[
            pltpu.VMEM((16, rows, cols), low),
            pltpu.VMEM((16, depth, q_cols + HD), low),
            pltpu.VMEM((16, 2 * span + LABEL_ROWS, HD), low),
            pltpu.VMEM((8, 2, 8, w_out.shape[0] // 8, w_out.shape[1]), low),
            pltpu.VMEM((16, rows, q_cols), low),
            pltpu.VMEM((16, rows, cols), low),
            pltpu.VMEM((8, UPPER, cols), low),
            pltpu.VMEM((2, 2, 4, rows - UPPER, cols), low),
            pltpu.VMEM((2, 3, UPPER, cols), low),
            pltpu.VMEM((2, UPPER // 2, cols), low),
            pltpu.VMEM((rows - UPPER, cols), low),
            pltpu.VMEM((rows, q_cols + HD), wide),
            pltpu.VMEM((rows, HD), wide),
            pltpu.VMEM((heads, rows, HD), low),
            pltpu.VMEM((rows, HD), low),
            pltpu.VMEM((2, 3, rows, HD), low),
            pltpu.VMEM((8, w_out.shape[0] // 8, w_out.shape[1]), low),
            pltpu.VMEM((rows, q_cols), low),
            pltpu.VMEM((rows, cols), wide),
            pltpu.VMEM((rows, HD), wide),
            pltpu.VMEM((LABEL_ROWS, HD), jnp.int32),
            pltpu.VMEM((rows, HD), wide),
            pltpu.VMEM((rows, HD), wide),
            pltpu.VMEM((16, 1, cols), wide),
            pltpu.VMEM((heads, rows, HD), wide),
            pltpu.VMEM((heads, rows, HD), wide),
            pltpu.VMEM((heads, rows, HD), wide),
            pltpu.SemaphoreType.DMA((8,)),
            pltpu.SemaphoreType.DMA(((span + rows) // HD,)),
            pltpu.SemaphoreType.DMA((1,)),
            pltpu.SemaphoreType.DMA((SENDS,)),
            pltpu.SemaphoreType.DMA((COPIES,)),
            pltpu.SemaphoreType.DMA((4,)),
        ],
        compiler_params=pltpu.CompilerParams(
            collective_id=0, has_side_effects=True, vmem_limit_bytes=58 << 20
        ),
        name="attention_block",
    )(stream, pending, w_query, w_key, w_value, w_out, old_keys, old_values,
      prefix_labels, stretch_labels, gain, freqs, offset)


def per_device(
    stream,
    pending,
    norm_gain,
    w_query,
    w_key,
    w_value,
    w_out,
    prefix_keys,
    prefix_values,
    prefix_segments,
    stretch_segments,
    stretch_offset,
):
    freqs = inverse_freqs(HD)
    return run_block(
        stream, pending, w_query, w_key, w_value, w_out, prefix_keys, prefix_values,
        prefix_segments, stretch_segments, norm_gain.reshape(-1, HD),
        jnp.asarray(np.concatenate([freqs, freqs])[None]), stretch_offset,
    )


def solution(mesh):
    in_specs = (
        P("ctx", "tp"),
        P("tp", "ctx", None),
        P(),
        P("ctx", "tp"),
        P("ctx", None),
        P("ctx", None),
        P("tp", "ctx"),
        P(None, "ctx", None),
        P(None, "ctx", None),
        P("ctx"),
        P("ctx"),
        P(),
    )
    return jax.shard_map(
        per_device, mesh=mesh, in_specs=in_specs, out_specs=P("ctx", "tp"), check_vma=False
    )
```

```python
import functools
import math

import jax
import jax.numpy as jnp
import numpy as np
from jax import lax
from jax.experimental import pallas as pl
from jax.experimental.pallas import tpu as pltpu
from jax.sharding import PartitionSpec as P

MESH = pl.DeviceIdType.MESH
HD = 128
ROPE_BASE = 500000.0
ROPE_FACTOR = 8.0
LOW_FREQ = 1.0
HIGH_FREQ = 4.0
INITIAL_SPAN = 8192.0
NORM_EPSILON = 1e-05
MASKED = -1e30
LABEL_ROWS = 16


def inverse_freqs(head_width):
    pair_index = np.arange(head_width // 2, dtype=np.float64)
    base_freq = ROPE_BASE ** (-2.0 * pair_index / head_width)
    wavelength = 2.0 * math.pi / base_freq
    smooth = (INITIAL_SPAN / wavelength - LOW_FREQ) / (HIGH_FREQ - LOW_FREQ)
    blended = (1.0 - smooth) * base_freq / ROPE_FACTOR + smooth * base_freq
    chosen = np.where(
        wavelength < INITIAL_SPAN / HIGH_FREQ,
        base_freq,
        np.where(wavelength > INITIAL_SPAN / LOW_FREQ, base_freq / ROPE_FACTOR, blended),
    )
    return chosen.astype(np.float32)


def coords():
    c = lax.axis_index("ctx")
    t = lax.axis_index("tp")
    return c // 4, (c // 2) % 2, c % 2, t // 2, t % 2


def ctx_of(y, xh, core):
    return (y * 2 + xh) * 2 + core


def tp_of(z, xl):
    return z * 2 + xl


def neighbours():
    y, xh, core, z, xl = coords()
    here = ctx_of(y, xh, core)
    mine = tp_of(z, xl)
    return {
        "z+": (here, tp_of((z + 1) % 8, xl)),
        "z-": (here, tp_of((z + 7) % 8, xl)),
        "xl": (here, tp_of(z, 1 - xl)),
        "y+": (ctx_of((y + 1) % 4, xh, core), mine),
        "y-": (ctx_of((y + 3) % 4, xh, core), mine),
        "xh": (ctx_of(y, 1 - xh, core), mine),
        "xd": (ctx_of(y, 1 - xh, core), tp_of(z, 1 - xl)),
        "sib": (ctx_of(y, xh, 1 - core), mine),
    }


def greet(devices):
    barrier = pltpu.get_barrier_semaphore()
    for device in devices:
        pl.semaphore_signal(barrier, inc=1, device_id=device, device_id_type=MESH)
    pl.semaphore_wait(barrier, len(devices))


class Copy:
    def __init__(self, net, k, sent, ref, device):
        self.root, self.shape = getattr(ref, "ref", ref), ref.shape
        self.net, self.k, self.sent, self.device = net, k, sent, device

    def handle(self):
        lead = (0,) * (len(self.root.shape) - len(self.shape))
        like = self.root.at[(*lead, *(pl.ds(0, n) for n in self.shape))]
        return pltpu.make_async_remote_copy(
            src_ref=like,
            dst_ref=like,
            send_sem=self.net.send_sem.at[self.sent],
            recv_sem=self.net.recv_sem.at[self.k],
            device_id=self.device,
            device_id_type=MESH,
        )

    def wait_recv(self):
        self.handle().wait_recv()

    def wait_send(self):
        self.handle().wait_send()


class Net:
    def __init__(self, links, send_sem, recv_sem):
        self.links, self.send_sem, self.recv_sem = links, send_sem, recv_sem
        self.count, self.under_way, self.spare, self.used = 0, [], [], 0

    def push(self, src, link, dst=None):
        k, self.count = self.count, self.count + 1
        if self.spare:
            sent = self.spare.pop(0)
        else:
            sent, self.used = self.used, self.used + 1
        device = self.links[link] if isinstance(link, str) else link
        pltpu.make_async_remote_copy(
            src_ref=src,
            dst_ref=src if dst is None else dst,
            send_sem=self.send_sem.at[sent],
            recv_sem=self.recv_sem.at[k],
            device_id=device,
            device_id_type=MESH,
        ).start()
        self.under_way.append(Copy(self, k, sent, src, device))
        return self.under_way[-1]

    def drain(self, before=None):
        done = [copy for copy in self.under_way if before is None or copy.k < before]
        self.under_way = [copy for copy in self.under_way if copy not in done]
        for copy in done:
            copy.wait_send()
        self.spare += [copy.sent for copy in done]


class TpRing:
    def __init__(self, net, own, buf, upper):
        self.net, self.own, self.buf = net, own, buf
        half = own.shape[0] - upper
        part = -(-upper // 32) * 16
        self.low, self.high = pl.ds(0, half), pl.ds(half, upper)
        self.parts = (pl.ds(half, part), pl.ds(half + part, upper - part))
        _, _, _, z, xl = coords()
        t = tp_of(z, xl)
        self.swap = net.push(own.at[self.low], "xl", buf.at[t, self.low])
        self.hop = {}
        for way in ("z+", "z-"):
            self.hop[way, "own"] = net.push(own.at[self.low], way, buf.at[t, self.low])
            self.hop[way, "high"] = net.push(own.at[self.high], way, buf.at[t, self.high])
        self.across = []

    def cross(self):
        _, _, _, z, xl = coords()
        self.swap.wait_recv()
        for way in ("z+", "z-"):
            self.hop[way, "other"] = self.net.push(self.buf.at[tp_of(z, 1 - xl), self.low], way)
        self.across.append(
            self.net.push(self.own.at[self.high], "xl", self.buf.at[tp_of(z, xl), self.high])
        )

    def step(self, step):
        _, _, _, z, xl = coords()
        push, buf, hop = self.net.push, self.buf, self.hop
        for kind in ("own", "high", "other"):
            for way, sign in (("z+", -1), ("z-", 1)):
                at = (z + sign * step + 8) % 8
                mine, theirs = tp_of(at, xl), tp_of(at, 1 - xl)
                part = 0 if way == "z+" else 1
                if kind == "high":
                    hop[way, kind].wait_recv()
                    if step < 4:
                        rows = self.high if step < 3 else self.parts[part]
                        hop[way, kind] = push(buf.at[mine, rows], way)
                    rows = self.high if step < 4 else self.parts[part]
                    self.across.append(push(buf.at[mine, rows], "xl"))
                    continue
                last = part == (0 if kind == "own" else 1)
                if step < 4 or last:
                    hop[way, kind].wait_recv()
                if step < 3 or (step == 3 and last):
                    hop[way, kind] = push(buf.at[mine if kind == "own" else theirs, self.low], way)

    def arrive(self, first, last):
        for copy in self.across[first:last]:
            copy.wait_recv()


class CtxRing:
    def __init__(self, net, own, slot, side_link):
        self.net, self.own, self.slot, self.side_link = net, own, slot, side_link
        y, xh, core, _, _ = coords()
        self.c, self.beside = ctx_of(y, xh, core), ctx_of(y, 1 - xh, core)
        self.sib, self.hop = [], {}

    def send_across(self):
        self.side = self.net.push(self.own, self.side_link, self.slot(self.c))
        self.sib.append(self.net.push(self.own, "sib", self.slot(self.c)))

    def send_own(self):
        for way in ("y+", "y-"):
            self.hop[way, "own"] = self.net.push(self.own, way, self.slot(self.c))

    def send_side(self):
        self.side.wait_recv()
        for way in ("y+", "y-"):
            self.hop[way, "side"] = self.net.push(self.slot(self.beside), way)
        self.sib.append(self.net.push(self.slot(self.beside), "sib"))

    def came(self, way, step, kind):
        y, xh, core, _, _ = coords()
        at = (y + (-step if way == "y+" else step) + 4) % 4
        self.hop[way, kind].wait_recv()
        return self.slot(ctx_of(at, xh if kind == "own" else 1 - xh, core))

    def near(self, kind):
        for way in ("y+", "y-"):
            block = self.came(way, 1, kind)
            if (way == "y+") == (kind == "own"):
                self.hop[way, kind] = self.net.push(block, way)
            self.sib.append(self.net.push(block, "sib"))

    def far(self):
        for way, kind in (("y+", "own"), ("y-", "side")):
            self.sib.append(self.net.push(self.came(way, 2, kind), "sib"))

    def finish(self):
        for copy in self.sib:
            copy.wait_recv()


class Turn:
    def __init__(self, net, w_out, mid, turned, sems):
        self.net, self.w_out, self.mid, self.turned, self.sems = net, w_out, mid, turned, sems
        y, xh, core, z, xl = coords()
        self.eighth = y * 2 + xh
        self.rows = w_out.shape[0] // 8
        self.stays = core == xl

    def place(self, ahead):
        _, _, core, z, xl = coords()
        at = (self.eighth + ahead) % 8
        return (at * 2 + xl, tp_of(z, core))

    def height(self, ahead):
        _, _, _, z, xl = coords()
        c = lax.axis_index("ctx")
        return (c, tp_of((z + ahead) % 8, xl))

    def first(self):
        src = self.w_out.at[pl.ds(pl.multiple_of(self.eighth * self.rows, self.rows), self.rows)]
        dst = self.mid.at[self.eighth]
        away = pltpu.make_async_remote_copy(
            src_ref=src,
            dst_ref=dst,
            send_sem=self.sems.at[0],
            recv_sem=self.sems.at[1],
            device_id=self.place(0),
            device_id_type=MESH,
        )
        return away, pltpu.make_async_copy(src, dst, self.sems.at[2])

    def spread(self):
        away, stay = self.first()
        pl.when(jnp.logical_not(self.stays))(away.start)
        pl.when(self.stays)(stay.start)
        self.got = []
        for ahead in range(1, 8):
            at = (self.eighth + ahead) % 8
            src = self.w_out.at[pl.ds(pl.multiple_of(at * self.rows, self.rows), self.rows)]
            self.got.append(self.net.push(src, self.place(ahead), self.mid.at[self.eighth]))

    def own(self, z):
        core = lax.axis_index("ctx") % 2
        return self.turned.at[z, core, self.eighth]

    def rise(self):
        away, stay = self.first()

        @pl.when(jnp.logical_not(self.stays))
        def _():
            away.wait_send()
            away.wait_recv()

        pl.when(self.stays)(stay.wait)
        for copy in self.got:
            copy.wait_recv()
        _, _, _, z, _ = coords()
        keep = pltpu.make_async_copy(self.mid.at[z], self.own(z), self.sems.at[3])
        keep.start()
        self.risen = [
            self.net.push(self.mid.at[(z + ahead) % 8], self.height(ahead), self.own(z))
            for ahead in range(1, 8)
        ]

    def finish(self):
        _, _, _, z, _ = coords()
        pltpu.make_async_copy(self.mid.at[z], self.own(z), self.sems.at[3]).wait()
        for copy in self.risen:
            copy.wait_recv()


class PendingSum:
    def __init__(
        self, net, pending, slabs, crossed, landed, landed_high, landed_parts, final, sems
    ):
        self.net, self.slabs, self.crossed = net, slabs, crossed
        self.landed, self.landed_high = landed, landed_high
        self.landed_parts, self.final = landed_parts, final
        _, _, _, self.z, self.xl = coords()
        rows, cols = slabs.shape[1:]
        upper, part = crossed.shape[1], landed_parts.shape[1]
        self.half = rows - upper
        self.low, self.high = pl.ds(0, self.half), pl.ds(self.half, upper)
        self.parts = (pl.ds(self.half, part), pl.ds(self.half + part, upper - part))
        self.loads = [
            pltpu.make_async_copy(
                pending.at[0, :, pl.ds(k * cols, cols)], slabs.at[k], sems.at[0]
            )
            for k in range(16)
        ]
        for load in self.loads:
            load.start()
        self.hop, self.over, self.sems = {}, {}, sems

    def at(self, offset, other=0):
        return tp_of((self.z + offset + 8) % 8, (self.xl + other) % 2)

    def ready(self):
        pltpu.make_async_copy(self.slabs, self.slabs, self.sems.at[0]).wait()

    def cross(self, *offsets):
        for offset in offsets:
            slot = (self.z + offset + 8) % 8
            self.over[offset] = self.net.push(
                self.slabs.at[self.at(offset, 1), self.high], "xl", self.crossed.at[slot]
            )

    def add(self, index, rows, more):
        total = self.slabs[index, rows].astype(jnp.float32) + more.astype(jnp.float32)
        self.slabs[index, rows] = total.astype(jnp.bfloat16)

    def take_crossed(self, offset):
        self.over[offset].wait_recv()
        slot = (self.z + offset + 8) % 8
        self.add(self.at(offset), self.high, self.crossed[slot])

    def land(self, way, kind, step):
        if kind == 2 and step == 0:
            return self.landed_parts.at[way]
        if kind == 2:
            return self.landed_high.at[way, step - 1]
        return self.landed.at[way, kind, step]

    def send(self, way, kind, step, index, rows):
        self.hop[way, kind] = self.net.push(
            self.slabs.at[index, rows], ("z+", "z-")[way], self.land(way, kind, step)
        )

    def first(self):
        self.send(0, 0, 0, self.at(4), self.low)
        self.send(1, 1, 0, self.at(4, 1), self.low)

    def first_high(self):
        self.take_crossed(4)
        for way in (0, 1):
            self.send(way, 2, 0, self.at(4), self.parts[way])

    def step(self, step, kinds):
        for way, sign in ((0, 1), (1, -1)):
            offset = sign * (4 - step)
            for kind in kinds:
                index = self.at(offset, 1 if kind == 1 else 0)
                rows = self.high if kind == 2 else self.low
                if kind == 2:
                    self.take_crossed(offset)
                if step > 1 or kind == 2 or kind == way:
                    self.hop[way, kind].wait_recv()
                    into = self.parts[way] if kind == 2 and step == 1 else rows
                    self.add(index, into, self.land(way, kind, step - 1)[...])
                self.send(way, kind, step, index, rows)

    def last_other(self):
        for way in (0, 1):
            self.hop[way, 1].wait_recv()
        more = self.landed[0, 1, 3].astype(jnp.float32) + self.landed[1, 1, 3].astype(jnp.float32)
        self.add(self.at(0, 1), self.low, more)
        self.fold = self.net.push(self.slabs.at[self.at(0, 1), self.low], "xl", self.final)

    def last(self):
        wide = jnp.float32
        for way in (0, 1):
            self.hop[way, 0].wait_recv()
            self.hop[way, 2].wait_recv()
        self.over[0].wait_recv()
        self.fold.wait_recv()
        low = self.slabs[self.at(0), self.low].astype(wide) + self.final[...].astype(wide)
        low = low + self.landed[0, 0, 3].astype(wide) + self.landed[1, 0, 3].astype(wide)
        high = self.slabs[self.at(0), self.high].astype(wide) + self.crossed[self.z].astype(wide)
        high = high + self.landed_high[0, 2].astype(wide) + self.landed_high[1, 2].astype(wide)
        return low, high


COPIES = 159
UPPER = 192
SENDS = 56


def block_kernel(
    stream, pending, w_query, w_key, w_value, w_out, old_keys, old_values,
    prefix_labels, stretch_labels, gain, freqs, offset,
    output,
    blocks, weights, cache, out_rows, gathered,
    slabs, crossed, landed, landed_high, landed_parts, final,
    totals, squares, query, made, fresh, mid, attended, total_out, q_marks, labels, cosine, sinus, gains,
    top, total, mix,
    local_sem, label_sem, load_sem, send_sem, recv_sem, turn_sem,
):
    y, xh, core, z, xl = coords()
    c, t = ctx_of(y, xh, core), tp_of(z, xl)
    rows = stream.shape[0]
    span = old_keys.shape[1]
    q_cols = w_query.shape[1]
    heads = q_cols // HD

    def row_of(marks, first, count):
        wide = marks.astype(jnp.float32)
        return jnp.concatenate([wide[first + k : first + k + 1] for k in range(count)], axis=1)

    def arrival(j):
        away = (j + 2) // 4
        sign = 1 - 2 * (((j + 2) // 2) % 2)
        return tp_of((z + sign * away + 8) % 8, (xl + j % 2) % 2)

    local = [
        pltpu.make_async_copy(stream, blocks.at[t], local_sem.at[0]),
        pltpu.make_async_copy(w_query, weights.at[c, :, pl.ds(0, q_cols)], local_sem.at[1]),
        pltpu.make_async_copy(old_keys.at[z], cache.at[c, pl.ds(0, span)], local_sem.at[2]),
        pltpu.make_async_copy(old_values.at[z], cache.at[c, pl.ds(span, span)], local_sem.at[3]),
    ]
    marks_here = [
        pltpu.make_async_copy(ref.at[pl.ds(k * HD, HD)], labels.at[row], label_sem.at[row])
        for ref, k, row in [(prefix_labels, k, k) for k in range(span // HD)]
        + [(stretch_labels, k, span // HD + k) for k in range(rows // HD)]
    ]
    head_cols = pl.ds(pl.multiple_of(z * HD, HD), HD)
    kv_slot = weights.at[c, :, pl.ds(q_cols, HD)]
    key_copy = pltpu.make_async_copy(w_key.at[:, head_cols], kv_slot, local_sem.at[5])
    value_copy = pltpu.make_async_copy(w_value.at[:, head_cols], kv_slot, local_sem.at[5])
    links = neighbours()
    later = {}
    for ahead in (1, 2):
        for other in (0, 1):
            later[ahead, other] = ((c + ahead) % 16, tp_of(z, (xl + other) % 2))
    earlier = [
        ((c + 16 - ahead) % 16, tp_of(z, (xl + other) % 2)) for ahead in (1, 2) for other in (0, 1)
    ]
    net = Net(links, send_sem, recv_sem)
    turn = Turn(net, w_out, mid, out_rows, turn_sem)
    peers = list(links.values()) + list(later.values()) + earlier
    peers += [turn.place(ahead) for ahead in range(1, 8)]
    peers += [turn.height(ahead) for ahead in range(2, 7)]
    barrier = pltpu.get_barrier_semaphore()
    for device in peers:
        pl.semaphore_signal(barrier, inc=1, device_id=device, device_id_type=MESH)

    labels[...] = jnp.zeros_like(labels)
    for copy in local + marks_here:
        copy.start()

    @pl.when(xl == 0)
    def _():
        key_copy.start()

    @pl.when(xl == 1)
    def _():
        value_copy.start()

    @pl.when(core != xl)
    def _():
        pl.semaphore_signal(barrier, inc=1, device_id=turn.place(0), device_id_type=MESH)
        pl.semaphore_wait(barrier, len(peers) + 1)

    @pl.when(core == xl)
    def _():
        pl.semaphore_wait(barrier, len(peers))

    tp_ring = TpRing(net, stream, blocks, 176)
    local[1].wait()
    key_copy.wait()
    w_ring = CtxRing(net, weights.at[c], lambda k: weights.at[k], "xh")
    w_ring.send_own()
    w_ring.send_across()
    for copy in local[2:] + marks_here:
        copy.wait()
    cache[c, 2 * span :] = labels[...].astype(jnp.float32).astype(jnp.bfloat16)
    old_ring = CtxRing(net, cache.at[c], lambda k: cache.at[k], "xd")
    out_ring = CtxRing(
        net, turn.own(pl.ds(0, 8)), lambda k: out_rows.at[:, k % 2, k // 2], "xh"
    )
    sums = PendingSum(net, pending, slabs, crossed, landed, landed_high, landed_parts, final, load_sem)
    row = row_of(cache[c, 2 * span :], span // HD, rows // HD)
    flat = (rows, rows)
    diagonal = lax.broadcasted_iota(jnp.int32, flat, 0) == lax.broadcasted_iota(jnp.int32, flat, 1)
    q_marks[...] = jnp.sum(jnp.where(diagonal, row, 0.0), axis=1, keepdims=True) + jnp.zeros(
        (rows, HD), jnp.float32
    )
    token = (c * rows + lax.broadcasted_iota(jnp.int32, (rows, HD), 0)).astype(jnp.float32)
    angles = (offset[0].astype(jnp.float32) + token) * freqs[...]
    turns = jnp.floor(angles * (0.5 / math.pi) + 0.5)
    angles = (angles - turns * 6.28125) - turns * (2.0 * math.pi - 6.28125)
    cosine[...] = jnp.cos(angles)
    lower = lax.broadcasted_iota(jnp.int32, (rows, HD), 1) < HD // 2
    sinus[...] = jnp.where(lower, -1.0, 1.0) * jnp.sin(angles)
    wide_gain = gain[...].astype(jnp.float32)
    per_block = stream.shape[1] // HD
    for b in range(16):
        gains[b] = row_of(wide_gain, b * per_block, per_block)
    totals[...] = jnp.zeros_like(totals)
    squares[...] = jnp.zeros_like(squares)
    tp_ring.cross()
    starts = net.count
    turn.spread()
    w_ring.near("own")
    tp_ring.step(1)
    w_ring.send_side()
    old_ring.send_across()
    first = net.count
    tp_ring.step(2)
    net.drain(starts)
    w_ring.near("side")
    w_ring.far()
    net.drain(first)
    early = net.count
    old_ring.send_own()
    old_ring.send_side()
    tp_ring.step(3)
    sums.ready()
    sums.cross(4)
    w_ring.finish()
    tp_ring.arrive(0, 5)
    local[0].wait()

    def project(j, _):
        b = arrival(j)
        wide = blocks[b].astype(jnp.float32)
        part = wide * wide
        squares[...] += sum(part[:, k * HD : (k + 1) * HD] for k in range(part.shape[1] // HD))
        low = (wide * gains[b]).astype(jnp.bfloat16)
        totals[...] += jnp.dot(low, weights[b], preferred_element_type=jnp.float32)
        return 0

    lax.fori_loop(0, 10, project, 0)
    tp_ring.step(4)
    net.drain(early)
    sums.first()
    sums.first_high()
    turn.rise()
    old_ring.near("own")
    tp_ring.arrive(5, 9)
    sums.cross(3, -3)
    lax.fori_loop(10, 16, project, 0)
    width = 16 * stream.shape[1]
    mean_square = jnp.sum(squares[...], axis=1, keepdims=True) / width
    scale = lax.rsqrt(mean_square + NORM_EPSILON)
    def rotate(part):
        return part * cosine[...] + pltpu.roll(part, HD // 2, 1) * sinus[...]

    part = totals[:, 2 * HD :] * scale

    @pl.when(xl == 0)
    def _():
        made[...] = rotate(part).astype(jnp.bfloat16)

    @pl.when(xl == 1)
    def _():
        made[...] = part.astype(jnp.bfloat16)

    keep = pltpu.make_async_copy(made, fresh.at[xl, 2], local_sem.at[7])
    keep.start()
    sent = [net.push(made, "xl", fresh.at[xl, 2])]
    for (ahead, _), device in later.items():
        sent.append(net.push(made, device, fresh.at[xl, 2 - ahead]))
    sums.step(1, (0, 1))

    to_exponent = math.log2(math.e) / math.sqrt(HD)
    for h in range(heads):
        part = totals[:, h * HD : (h + 1) * HD] * scale
        query[h] = (rotate(part) * to_exponent).astype(jnp.bfloat16)

    net.drain(early)
    sent_before = net.count
    top[...] = jnp.full_like(top, MASKED)
    total[...] = jnp.zeros_like(total)
    mix[...] = jnp.zeros_like(mix)
    own_marks = q_marks[:, :1]

    def absorb(h, keys, values, seen):
        scores = lax.dot_general(
            query[h], keys, (((1,), (1,)), ((), ())), preferred_element_type=jnp.float32
        )
        scores = jnp.where(seen, scores, MASKED)
        before = top[h]
        now = jnp.maximum(before, jnp.max(scores, axis=1, keepdims=True))
        fade = jnp.exp2(before - now)
        shares = jnp.exp2(scores - now[:, :1])
        total[h] = total[h] * fade + jnp.sum(shares, axis=1, keepdims=True)
        mix[h] = mix[h] * fade + jnp.dot(
            shares.astype(jnp.bfloat16), values, preferred_element_type=jnp.float32
        )
        top[h] = now

    def over_prefix(i, _):
        def on(k, *actions):
            @pl.when(i == k)
            def _():
                for action in actions:
                    action()

        for k in range(16):
            if k in before_block:
                on(k, *before_block[k])
        group, beside = i // 4, (i // 2) % 2
        turn_y = jnp.where(group == 0, 0, jnp.where(group == 3, 2, 3 - 2 * beside))
        turn_x = jnp.where(group == 1, 0, jnp.where(group == 2, 1, beside))
        at = ctx_of((y + turn_y) % 4, (xh + turn_x) % 2, (core + i % 2) % 2)
        marks = row_of(cache[at, 2 * span :], 0, span // HD)
        seen = marks <= own_marks
        for h in range(heads):
            absorb(h, cache[at, :span], cache[at, span : 2 * span], seen)
        return 0

    def sib(ring, *numbers):
        def wait():
            for k in numbers:
                ring.sib[k].wait_recv()

        return wait

    def start_out():
        turn.finish()
        out_ring.send_own()
        out_ring.send_across()

    before_block = {
        0: [sib(old_ring, 0, 1)],
        1: [lambda: sums.cross(2, -2)],
        4: [lambda: sums.step(1, (2,)), lambda: old_ring.near("side"), sib(old_ring, 2, 3)],
        5: [turn.finish, out_ring.send_across],
        6: [lambda: sums.step(2, (0, 1)), old_ring.far],
        7: [out_ring.send_own],
        8: [sib(old_ring, 4, 5)],
        9: [lambda: net.drain(sent_before), lambda: sums.step(2, (2,)), lambda: sums.cross(1, -1, 0)],
        11: [lambda: sums.step(3, (0, 1))],
        12: [sib(old_ring, 6, 7)],
        13: [out_ring.send_side],
        14: [lambda: out_ring.near("own")],
        15: [lambda: sums.step(3, (2,))],
    }
    lax.fori_loop(0, 16, over_prefix, 0)
    for copy in sent:
        copy.wait_recv()
    keep.wait()
    out_ring.near("side")
    for j in range(3):
        back = 2 - j
        row = row_of(cache[(c + 16 - back) % 16, 2 * span :], span // HD, rows // HD)
        row = jnp.where(c >= back, row, -1.0)
        same = row == own_marks
        if back == 0:
            at = lax.broadcasted_iota(jnp.int32, (rows, rows), 0)
            key_at = lax.broadcasted_iota(jnp.int32, (rows, rows), 1)
            same = same & (key_at <= at)
        for h in range(heads):
            absorb(h, fresh[0, j], fresh[1, j], same)
    for h in range(heads):
        attended[:, h * HD : (h + 1) * HD] = (mix[h] / total[h]).astype(jnp.bfloat16)

    net.drain(net.count - 16)
    ring = TpRing(net, attended, gathered, 208)
    gathered[t] = attended[...]
    ring.cross()
    sums.last_other()
    out_ring.far()
    ring.step(1)
    out_ring.finish()
    low, high = sums.last()
    total_out[: sums.half] = low + blocks[t, : sums.half].astype(jnp.float32)
    total_out[sums.half :] = high + blocks[t, sums.half :].astype(jnp.float32)

    def project_out(j, _):
        b = arrival(j)
        part = out_rows[b // 2, b % 2].reshape(q_cols, stream.shape[1])
        total_out[...] += jnp.dot(gathered[b], part, preferred_element_type=jnp.float32)
        return 0

    ring.arrive(0, 1)
    lax.fori_loop(0, 2, project_out, 0)
    ring.step(2)
    ring.arrive(1, 3)
    lax.fori_loop(2, 6, project_out, 0)
    ring.step(3)
    ring.arrive(3, 5)
    lax.fori_loop(6, 10, project_out, 0)
    ring.step(4)
    ring.arrive(5, 7)
    lax.fori_loop(10, 14, project_out, 0)
    ring.arrive(7, 9)
    lax.fori_loop(14, 16, project_out, 0)
    output[...] = total_out[...].astype(jnp.bfloat16)
    net.drain()
    assert net.count == COPIES and net.used == SENDS, (net.count, net.used)


def run_block(stream, pending, w_query, w_key, w_value, w_out, old_keys, old_values,
              prefix_labels, stretch_labels, gain, freqs, offset):
    rows, cols = stream.shape
    depth, q_cols = w_query.shape
    span = old_keys.shape[1]
    low, wide = jnp.bfloat16, jnp.float32
    any_spec = pl.BlockSpec(memory_space=pl.ANY)
    vmem = pl.BlockSpec(memory_space=pltpu.VMEM)
    heads = q_cols // HD
    return pl.pallas_call(
        block_kernel,
        out_shape=jax.ShapeDtypeStruct((rows, cols), low),
        in_specs=[any_spec] * 10 + [vmem] * 2 + [pl.BlockSpec(memory_space=pltpu.SMEM)],
        out_specs=vmem,
        scratch_shapes=[
            pltpu.VMEM((16, rows, cols), low),
            pltpu.VMEM((16, depth, q_cols + HD), low),
            pltpu.VMEM((16, 2 * span + LABEL_ROWS, HD), low),
            pltpu.VMEM((8, 2, 8, w_out.shape[0] // 8, w_out.shape[1]), low),
            pltpu.VMEM((16, rows, q_cols), low),
            pltpu.VMEM((16, rows, cols), low),
            pltpu.VMEM((8, UPPER, cols), low),
            pltpu.VMEM((2, 2, 4, rows - UPPER, cols), low),
            pltpu.VMEM((2, 3, UPPER, cols), low),
            pltpu.VMEM((2, UPPER // 2, cols), low),
            pltpu.VMEM((rows - UPPER, cols), low),
            pltpu.VMEM((rows, q_cols + HD), wide),
            pltpu.VMEM((rows, HD), wide),
            pltpu.VMEM((heads, rows, HD), low),
            pltpu.VMEM((rows, HD), low),
            pltpu.VMEM((2, 3, rows, HD), low),
            pltpu.VMEM((8, w_out.shape[0] // 8, w_out.shape[1]), low),
            pltpu.VMEM((rows, q_cols), low),
            pltpu.VMEM((rows, cols), wide),
            pltpu.VMEM((rows, HD), wide),
            pltpu.VMEM((LABEL_ROWS, HD), jnp.int32),
            pltpu.VMEM((rows, HD), wide),
            pltpu.VMEM((rows, HD), wide),
            pltpu.VMEM((16, 1, cols), wide),
            pltpu.VMEM((heads, rows, HD), wide),
            pltpu.VMEM((heads, rows, HD), wide),
            pltpu.VMEM((heads, rows, HD), wide),
            pltpu.SemaphoreType.DMA((8,)),
            pltpu.SemaphoreType.DMA(((span + rows) // HD,)),
            pltpu.SemaphoreType.DMA((1,)),
            pltpu.SemaphoreType.DMA((SENDS,)),
            pltpu.SemaphoreType.DMA((COPIES,)),
            pltpu.SemaphoreType.DMA((4,)),
        ],
        compiler_params=pltpu.CompilerParams(
            collective_id=0, has_side_effects=True, vmem_limit_bytes=58 << 20
        ),
        name="attention_block",
    )(stream, pending, w_query, w_key, w_value, w_out, old_keys, old_values,
      prefix_labels, stretch_labels, gain, freqs, offset)


def per_device(
    stream,
    pending,
    norm_gain,
    w_query,
    w_key,
    w_value,
    w_out,
    prefix_keys,
    prefix_values,
    prefix_segments,
    stretch_segments,
    stretch_offset,
):
    freqs = inverse_freqs(HD)
    return run_block(
        stream, pending, w_query, w_key, w_value, w_out, prefix_keys, prefix_values,
        prefix_segments, stretch_segments, norm_gain.reshape(-1, HD),
        jnp.asarray(np.concatenate([freqs, freqs])[None]), stretch_offset,
    )


def solution(mesh):
    in_specs = (
        P("ctx", "tp"),
        P("tp", "ctx", None),
        P(),
        P("ctx", "tp"),
        P("ctx", None),
        P("ctx", None),
        P("tp", "ctx"),
        P(None, "ctx", None),
        P(None, "ctx", None),
        P("ctx"),
        P("ctx"),
        P(),
    )
    return jax.shard_map(
        per_device, mesh=mesh, in_specs=in_specs, out_specs=P("ctx", "tp"), check_vma=False
    )
```
